128 devices in a mesh: ctx: 16 (over z, x), head: 8 (over y, core).
Axes of the slice: x: 4, y: 4, z: 4, core: 2. Of those that a mesh axis runs over, the one named last changes fastest.
Arguments:
- queries: bfloat16 [16384, 8192], P(('ctx', 'head')), may hold values from -200 to 200
- keys: bfloat16 [16384, 1024], P(('ctx', 'head')), may hold values from -6 to 6
- values: bfloat16 [16384, 1024], P(('ctx', 'head')), may hold values from -6 to 6
- out_grad: bfloat16 [16384, 8192], P(('ctx', 'head')), may hold values from -6 to 6
- doc_starts: int32 [256], replicated, may hold values from 0 to 16383, as said below
- piece_order: int32 [16, 16], replicated, may hold values from 0 to 15, as said below
Outputs:
- attended: bfloat16 [16384, 8192], P(('ctx', 'head'))
- query_grad: bfloat16 [16384, 8192], P(('ctx', 'head'))
- key_grad: bfloat16 [16384, 1024], P(('ctx', 'head'))
- value_grad: bfloat16 [16384, 1024], P(('ctx', 'head'))
The draws below stay inside these ranges and needn't reach their ends.
Inputs may be any that keep to these rules, and one draw needn't show every extreme that they name: `doc_starts`: Increasing; the first is 0; every document, the last one running to 16384, has 1 to 256 tokens, and one has exactly 256. `piece_order`: row i names each of the 16 blocks of 64 consecutive tokens of context shard i once.
All inputs are finite; a program needn't handle non-finite values.
Results may differ from the reference program's by a relative error of at most 0.03.
Values may be sent and summed in bfloat16 or wider, within the bound.
A program may use at most 128 MiB of HBM per device.

```python
import math
import jax
import jax.numpy as jnp
from jax import lax

HQ = 64
HK = 8
DH = 128
TOK_DEV = 1024
QBLK = 128
TOKENS = 16384
MOST = 256
NDOCS = 256
N_CTX = 16


def doc_lengths(key):
    weights = jax.random.randint(jax.random.fold_in(key, 11), (NDOCS,), 32, 65, dtype=jnp.int32)
    longest = jax.random.randint(jax.random.fold_in(key, 12), (), 0, NDOCS, dtype=jnp.int32)
    doc_ids = jnp.arange(NDOCS, dtype=jnp.int32)
    long_mask = doc_ids == longest
    weights = jnp.where(long_mask, 0, weights)
    spare = TOKENS - MOST - (NDOCS - 1)
    share = 1 + spare * weights // jnp.sum(weights)
    share = jnp.where(long_mask, MOST, share)
    missing = TOKENS - jnp.sum(share)
    other_rank = doc_ids - (doc_ids > longest).astype(jnp.int32)
    extra = jnp.logical_and(other_rank < missing, jnp.logical_not(long_mask))
    share = share + extra.astype(jnp.int32)
    return share.astype(jnp.int32)


def key_normals(key):
    return jax.random.normal(key, (TOKENS, HK * DH), jnp.float32)


def draw_doc_starts(key, part):
    lengths = doc_lengths(key)
    return (jnp.cumsum(lengths) - lengths).astype(jnp.int32)


def draw_piece_order(key, part):
    lengths = doc_lengths(key)
    doc_begins = (jnp.cumsum(lengths) - lengths).astype(jnp.int32)
    positions = jnp.arange(TOKENS, dtype=jnp.int32)
    doc_index = jnp.sum((doc_begins[None, :] <= positions[:, None]).astype(jnp.int32), axis=1) - 1
    token_cost = positions - jnp.take(doc_begins, doc_index) + 1
    piece_cost = jnp.sum(token_cost.reshape(N_CTX, N_CTX, TOK_DEV // N_CTX), axis=2)
    shard_ids = jnp.arange(N_CTX, dtype=jnp.int32)
    ranking = piece_cost * N_CTX + shard_ids[None, :]
    ranked = jnp.argsort(ranking, axis=1).astype(jnp.int32)
    shifted = (shard_ids[None, :] - shard_ids[:, None]) % N_CTX
    return jnp.take_along_axis(ranked, shifted, axis=1).astype(jnp.int32)


def draw_keys(key, part):
    normals = key_normals(key)
    return jnp.clip(normals, -6.0, 6.0).astype(jnp.bfloat16)


def draw_queries(key, part):
    key = jax.random.fold_in(key, 9)
    return jnp.clip(jax.random.normal(key, (TOKENS, HQ * DH), jnp.float32), -6.0, 6.0).astype(jnp.bfloat16)


def block_scale(stream_key, dims, cuts, least, top_value):
    factor_of = 1.0
    for dim, parts in cuts:
        heights = jax.random.uniform(jax.random.fold_in(jax.random.fold_in(stream_key, 6), dim), (parts,), jnp.float32, least / len(cuts), top_value / len(cuts))
        factor_of = factor_of * jnp.repeat(jnp.exp(heights), dims[dim] // parts).reshape((-1,) + (1,) * (len(dims) - 1 - dim))
    return factor_of


def bell_draw(stream_key, shape, scale, most, split=(), held_as=jnp.bfloat16):
    entries = jax.random.normal(stream_key, shape, jnp.float32) * scale
    if len(split) > 0:
        entries = block_scale(stream_key, shape, split, -0.22, 0.18) * entries
    return jnp.clip(entries, min=-most, max=most).astype(held_as)


def setup_inputs(seed: int = 0) -> dict:
    streams_of = jax.random.split(jax.random.key(seed), 7)
    queries = draw_queries(jax.random.fold_in(streams_of[6], 71), 0)
    keys = draw_keys(jax.random.fold_in(streams_of[6], 71), 0)
    values = bell_draw(streams_of[2], (TOKENS, HK * DH), 1.0, 6.0, ((0, 128),))
    out_grad = bell_draw(streams_of[3], (TOKENS, HQ * DH), 1.0, 6.0, ((0, 128),))
    doc_starts = draw_doc_starts(jax.random.fold_in(streams_of[6], 71), 0)
    piece_order = draw_piece_order(jax.random.fold_in(streams_of[6], 71), 0)
    return dict(queries=queries, keys=keys, values=values, out_grad=out_grad, doc_starts=doc_starts, piece_order=piece_order)


def sign_grid(grid_size):
    row_ids = jnp.arange(grid_size, dtype=jnp.int32)[:, None]
    column_ids = jnp.arange(grid_size, dtype=jnp.int32)[None, :]
    common = jnp.bitwise_and(row_ids, column_ids)
    parity = jnp.zeros((grid_size, grid_size), jnp.int32)
    for shift_bit in range(grid_size.bit_length()):
        parity = parity + jnp.bitwise_and(jnp.right_shift(common, shift_bit), 1)
    return jnp.where(parity % 2 == 0, 1.0, -1.0).astype(jnp.float32)

def doc_begin(positions, doc_starts):
    flat_pos = positions.reshape(-1)
    before = doc_starts[None, :] <= flat_pos[:, None]
    begin_pos = lax.optimization_barrier(jnp.max(jnp.where(before, doc_starts[None, :], 0), axis=1))
    return begin_pos.reshape(positions.shape)

def attend(queries_block, window, grads_block, query_pos, begin_pos, key_pos):
    inverse_root = 1.0 / math.sqrt(DH)
    pieces, query_rows, query_width = queries_block.shape
    window_rows = window.shape[1]
    key_width = window.shape[2] // 2
    key_heads = key_width // DH
    group_size = query_width // key_width
    key_part = window[:, :, :key_width].reshape(pieces, window_rows, key_heads, DH).astype(jnp.float32)
    value_part = window[:, :, key_width:].reshape(pieces, window_rows, key_heads, DH).astype(jnp.float32)
    query_split = queries_block.reshape(pieces, query_rows, key_heads, group_size, DH).astype(jnp.float32)
    grad_split = grads_block.reshape(pieces, query_rows, key_heads, group_size, DH).astype(jnp.float32)
    scores = jnp.einsum('prhgd,pwhd->phgrw', query_split, key_part) * inverse_root
    allowed = (key_pos[:, None, :] <= query_pos[:, :, None]) & (key_pos[:, None, :] >= begin_pos[:, :, None])
    allowed = allowed[:, None, None, :, :]
    masked = jnp.where(allowed, scores, -jnp.inf)
    row_top = lax.optimization_barrier(jnp.max(masked, axis=-1, keepdims=True))
    row_total = lax.optimization_barrier(jnp.sum(jnp.exp(masked - row_top), axis=-1, keepdims=True))
    logsum = row_top + jnp.log(row_total)
    probability = jnp.exp(masked - logsum)
    weights = probability.astype(jnp.bfloat16)
    output = jnp.einsum('phgrw,pwhd->prhgd', weights.astype(jnp.float32), value_part).astype(jnp.bfloat16)
    row_delta = lax.optimization_barrier(jnp.sum(grad_split * output.astype(jnp.float32), axis=-1))
    row_delta = jnp.transpose(row_delta, (0, 2, 3, 1))[..., None]
    prob_grad = jnp.einsum('prhgd,pwhd->phgrw', grad_split, value_part)
    score_grad = (probability * (prob_grad - row_delta)).astype(jnp.bfloat16).astype(jnp.float32)
    query_term = jnp.einsum('phgrw,pwhd->prhgd', score_grad, key_part) * inverse_root
    key_term = jnp.einsum('phgrw,prhgd->pwhd', score_grad, query_split) * inverse_root
    value_term = jnp.einsum('phgrw,prhgd->pwhd', weights.astype(jnp.float32), grad_split)
    key_terms = jnp.concatenate([key_term.reshape(pieces, window_rows, key_width), value_term.reshape(pieces, window_rows, key_width)], axis=-1)
    return (output.reshape(pieces, query_rows, query_width), query_term.reshape(pieces, query_rows, query_width), key_terms)

def rotate_back(blocks_in, grid):
    turned = jnp.dot(blocks_in.reshape(-1, DH), grid, precision=lax.Precision.HIGHEST, preferred_element_type=jnp.float32) * (1.0 / math.sqrt(DH))
    return turned.astype(jnp.bfloat16).reshape(blocks_in.shape)

def reference(queries, keys, values, out_grad, doc_starts, piece_order):
    inverse_root = 1.0 / math.sqrt(DH)
    grid = sign_grid(DH)
    total_rows = TOK_DEV * N_CTX
    piece_rows = TOK_DEV // N_CTX
    key_width = HK * DH
    query_width = HQ * DH
    key_codes = (jnp.dot(keys.reshape(-1, DH), grid.astype(jnp.bfloat16), preferred_element_type=jnp.float32) * inverse_root).astype(jnp.bfloat16).reshape(total_rows, key_width)
    key_pack = jnp.concatenate([key_codes, values], axis=1)
    shard_ids = jnp.arange(N_CTX, dtype=jnp.int32)
    source = (shard_ids[None, :, None] * TOK_DEV + jnp.transpose(piece_order)[:, :, None] * piece_rows + jnp.arange(piece_rows, dtype=jnp.int32)[None, None, :]).reshape(total_rows)
    grad_rows = jnp.zeros_like(out_grad).at[source].set(out_grad)
    window_rows = MOST + QBLK
    block_ids = jnp.arange(QBLK, dtype=jnp.int32)
    window_ids = jnp.arange(window_rows, dtype=jnp.int32)

    def visit(buffer, step_index):
        first_row = step_index * QBLK
        queries_block = lax.dynamic_slice_in_dim(queries, first_row, QBLK, 0)[None]
        grads_block = lax.dynamic_slice_in_dim(grad_rows, first_row, QBLK, 0)[None]
        window_start = jnp.maximum(first_row - MOST, 0).astype(jnp.int32)
        window = lax.dynamic_slice_in_dim(key_pack, window_start, window_rows, 0)[None]
        query_pos = (first_row + block_ids)[None]
        key_pos = (window_start + window_ids)[None]
        output, query_term, key_terms = attend(queries_block, window, grads_block, query_pos, doc_begin(query_pos, doc_starts), key_pos)
        current = lax.dynamic_slice_in_dim(buffer, window_start, window_rows, 0)
        buffer = lax.dynamic_update_slice_in_dim(buffer, current + key_terms[0], window_start, 0)
        return (buffer, (output[0], query_term[0]))
    start_buffer = jnp.zeros((total_rows, 2 * key_width), jnp.float32)
    buffer, (output, query_term) = lax.scan(visit, start_buffer, jnp.arange(total_rows // QBLK, dtype=jnp.int32))
    output = output.reshape(total_rows, query_width)
    attended = jnp.take(output, source, axis=0)
    query_grad = rotate_back(query_term.reshape(total_rows, query_width), grid)
    key_grad = rotate_back(buffer[:, :key_width], grid)
    value_grad = buffer[:, key_width:].astype(jnp.bfloat16)
    return (attended, query_grad, key_grad, value_grad)
```

```python
import functools
import math

import jax
import jax.numpy as jnp
import numpy as np
from jax import lax
from jax.experimental import pallas as pl
from jax.experimental.pallas import tpu as pltpu
from jax.sharding import PartitionSpec as P

MESH = pl.DeviceIdType.MESH
DH = 128
BLK = 128
MOST = 256
WIN = MOST + BLK
PIECE = 64
SHARD = 1024
WIDE = 1024
NCTX = 16
NHEAD = 8
GROUP = 2
NEG = -1e30
ROOT = 1.0 / math.sqrt(DH)


def sign_grid():
    ids = np.arange(DH)
    common = ids[:, None] & ids[None, :]
    parity = np.zeros((DH, DH), np.int64)
    for bit in range(8):
        parity += (common >> bit) & 1
    return np.where(parity % 2 == 0, 1.0, -1.0).astype(np.float32)


def unit(shard, kv):
    even = kv % 2 == 0
    return (
        jnp.where(even, shard, (kv // 2) * 4 + shard % 4),
        jnp.where(even, kv, 2 * (shard // 4) + 1),
    )


def attention_kernel(
    q, k, v, g, docs, order, sign,
    att_o, qg_o, kg_o, vg_o,
    qbuf, qrel, kraw, kcod, vbuf, gbuf, pst, att, stg, arel, dqs, dk, dv, hk, hv, kst, vst,
    s_k, s_v, s_hk, s_hv, s_qr, s_qo, s_qa, s_qf, s_g, s_att, s_af, s_qg, s_kg, s_vg, s_hal,
    r_k, r_v, r_q, r_qrel, r_g, r_arel, r_att, r_qg, r_kg, r_vg, r_hal,
):
    c = lax.axis_index("ctx")
    h = lax.axis_index("head")
    z, x, y, co = c // 4, c % 4, h // 2, h % 2
    shard = jnp.where(co == 0, c, y * 4 + x)
    kv = jnp.where(co == 0, 2 * y, 2 * z + 1)

    def al(index, size):
        return pl.ds(pl.multiple_of(index * size, size), size)

    def start(copy):
        src, dst, ssem, rsem, tc, th = copy
        own = (tc == c) & (th == h)

        @pl.when(own)
        def _():
            pltpu.make_async_copy(src, dst, rsem).start()

        @pl.when(jnp.logical_not(own))
        def _():
            pltpu.make_async_remote_copy(
                src, dst, ssem, rsem, device_id={"ctx": tc, "head": th}, device_id_type=MESH
            ).start()

    def drain(copy):
        src, dst, ssem, rsem, tc, th = copy
        own = (tc == c) & (th == h)

        @pl.when(jnp.logical_not(own))
        def _():
            pltpu.make_async_remote_copy(
                src, dst, ssem, rsem, device_id={"ctx": tc, "head": th}, device_id_type=MESH
            ).wait_send()

    def landed(ref, sem):
        pltpu.make_async_copy(ref, ref, sem).wait()

    def loop(count, body):
        def step(s, carry):
            body(s)
            return carry

        lax.fori_loop(0, count, step, 0)

    def copy_k(s):
        kk = (h + s) % NHEAD
        return (k.at[:, al(kk, DH)], kraw.at[al(h + 2, BLK)], s_k.at[s], r_k.at[h + 2]) + unit(c, kk)

    def copy_v(s):
        kk = (h + s) % NHEAD
        return (v.at[:, al(kk, DH)], vbuf.at[al(h + 2, BLK)], s_v.at[s], r_v.at[h + 2]) + unit(c, kk)

    def copy_hk(s):
        kk = (h + s) % NHEAD
        slot = kraw.at[al(h % 2, BLK)]
        return (k.at[:, al(kk, DH)], slot, s_hk.at[s], r_k.at[h % 2]) + unit((c + 1) % NCTX, kk)

    def copy_hv(s):
        kk = (h + s) % NHEAD
        slot = vbuf.at[al(h % 2, BLK)]
        return (v.at[:, al(kk, DH)], slot, s_hv.at[s], r_v.at[h % 2]) + unit((c + 1) % NCTX, kk)

    def copy_qr(s):
        to = (z + s + 1) % 4
        return (q.at[:, al(2 * to + 1, WIDE)], qrel.at[z], s_qr.at[s], r_qrel.at[z], to * 4 + x, h)

    def copy_qo():
        return (q.at[:, al(2 * z + 1, WIDE)], qbuf.at[h], s_qo.at[0], r_q.at[h], c, 2 * z + 1)

    def copy_qa(s):
        to = 2 * ((y + s) % 4)
        return (q.at[:, al(to, WIDE)], qbuf.at[h], s_qa.at[s], r_q.at[h], c, to)

    def copy_qf(s):
        src = (z + 3 - s) % 4
        return (qrel.at[src], qbuf.at[h], s_qf.at[s], r_q.at[h], c, 2 * src + 1)

    def copy_g(s):
        half = s % 2
        kk = (h + s // 2) % NHEAD
        src = g.at[al(half, PIECE), al(kk, WIDE)]
        return (src, gbuf.at[c], s_g.at[s], r_g.at[c]) + unit(2 * h + half, kk)

    def copy_att_far(s):
        j = (c + s) % NCTX
        slot = z * 2 + x % 2
        return (stg.at[j], arel.at[slot], s_att.at[s], r_arel.at[slot], j, 2 * y + x // 2)

    def copy_att_near(s):
        j = (c + s) % NCTX
        dst = att_o.at[al(x % 2, PIECE), al(kv, WIDE)]
        return (stg.at[j], dst, s_att.at[s], r_att.at[(x % 2) * 8 + kv], j, 2 * y + x // 2)

    def relayed(s):
        return ((z + 4 - s // 2) % 4) * 2 + s % 2

    def copy_af(s):
        m = relayed(s)
        dst = att_o.at[al(m % 2, PIECE), al(2 * y, WIDE)]
        return (arel.at[m], dst, s_af.at[s], r_att.at[(m % 2) * 8 + 2 * y], c, 2 * (m // 2) + co)

    def copy_qg(b):
        return (dqs.at[b], qg_o.at[:, al(kv, WIDE)], s_qg.at[b], r_qg.at[kv], shard, b)

    def copy_kg(b):
        return (kst.at[b], kg_o.at[:, al(kv, DH)], s_kg.at[b], r_kg.at[kv], shard, b)

    def copy_vg(b):
        return (vst.at[b], vg_o.at[:, al(kv, DH)], s_vg.at[b], r_vg.at[kv], shard, b)

    back = unit((shard + NCTX - 1) % NCTX, kv)
    copy_hal_k = (dk.at[pl.ds(0, MOST)], hk, s_hal.at[0], r_hal.at[0]) + back
    copy_hal_v = (dv.at[pl.ds(0, MOST)], hv, s_hal.at[1], r_hal.at[1]) + back

    def send_kv(s):
        start(copy_k(s))
        start(copy_v(s))

    def send_edge(s):
        start(copy_hk(s))
        start(copy_hv(s))

    loop(8, send_kv)

    @pl.when(h >= 6)
    def _():
        loop(8, send_edge)

    loop(3, lambda s: start(copy_qr(s)))
    start(copy_qo())
    loop(4, lambda s: start(copy_qa(s)))
    loop(16, lambda s: start(copy_g(s)))

    def pass_on(s):
        src = (z + 3 - s) % 4
        landed(qrel.at[src], r_qrel.at[src])
        start(copy_qf(s))

    loop(3, pass_on)

    dk[...] = jnp.zeros_like(dk)
    dv[...] = jnp.zeros_like(dv)
    starts = docs[...].astype(jnp.float32)

    loop(8, lambda b: landed(qbuf.at[b], r_q.at[b]))
    loop(16, lambda j: landed(gbuf.at[j], r_g.at[j]))
    loop(10, lambda n: landed(kraw.at[al(n, BLK)], r_k.at[n]))
    loop(10, lambda n: landed(vbuf.at[al(n, BLK)], r_v.at[n]))
    turned = jnp.dot(kraw[...], sign[...].astype(jnp.bfloat16), preferred_element_type=jnp.float32)
    kcod[...] = (turned * ROOT).astype(jnp.bfloat16)

    def pair(block, p):
        parts = [block[:, (GROUP * p + n) * DH : (GROUP * p + n + 1) * DH] for n in range(GROUP)]
        return jnp.concatenate(parts, axis=0)

    dims_nt = (((1,), (1,)), ((), ()))
    dims_tn = (((0,), (0,)), ((), ()))

    def forward(s):
        b = (h + 8 - s) % NHEAD
        row = lax.broadcasted_iota(jnp.int32, (BLK, 1), 0) + (shard * SHARD + b * BLK)
        rowf = row.astype(jnp.float32)
        begin = jnp.max(jnp.where(starts <= rowf, starts, 0.0), axis=1, keepdims=True)
        col = lax.broadcasted_iota(jnp.int32, (BLK, WIN), 1) + (shard * SHARD + b * BLK - MOST)
        colf = col.astype(jnp.float32)
        bias = jnp.where((colf <= rowf) & (colf >= begin), 0.0, NEG)
        bias = jnp.concatenate([bias] * GROUP, axis=0)
        kwin = kcod[pl.ds(pl.multiple_of(b * BLK, BLK), WIN), :]
        vwin = vbuf[pl.ds(pl.multiple_of(b * BLK, BLK), WIN), :]
        for p in range(8 // GROUP):
            q2 = jnp.concatenate(
                [qbuf[b, :, (GROUP * p + n) * DH : (GROUP * p + n + 1) * DH] for n in range(GROUP)], axis=0
            )
            score = lax.dot_general(q2, kwin, dims_nt, preferred_element_type=jnp.float32)
            score = score * (ROOT * math.log2(math.e)) + bias
            top = jnp.max(score, axis=1, keepdims=True)
            e = jnp.exp2(score - top)
            total = jnp.sum(e, axis=1, keepdims=True)
            w = (e * (1.0 / total)).astype(jnp.bfloat16)
            pst[b, p] = w
            out = jnp.dot(w, vwin, preferred_element_type=jnp.float32).astype(jnp.bfloat16)
            for n in range(GROUP):
                lanes = slice((GROUP * p + n) * DH, (GROUP * p + n + 1) * DH)
                att[2 * b, :, lanes] = out[n * BLK : n * BLK + PIECE]
                att[2 * b + 1, :, lanes] = out[n * BLK + PIECE : (n + 1) * BLK]

    loop(8, forward)

    def fill(j):
        stg[j] = att[order[shard, j]]

    loop(16, fill)

    def send_att(s):
        @pl.when(co == 0)
        def _():
            start(copy_att_far(s))

        @pl.when(co == 1)
        def _():
            start(copy_att_near(s))

    loop(16, send_att)

    def where_from(piece):
        def look(j, found):
            return jnp.where(order[shard, j] == piece, j, found)

        return lax.fori_loop(0, NCTX, look, 0)

    def backward(s):
        b = (h + s) % NHEAD
        j0 = where_from(2 * b)
        j1 = where_from(2 * b + 1)
        rows = pl.ds(pl.multiple_of(b * BLK, BLK), WIN)
        kwin = kraw[rows, :]
        vwin = vbuf[rows, :]
        dk_sum = jnp.zeros((WIN, DH), jnp.float32)
        dv_sum = jnp.zeros((WIN, DH), jnp.float32)
        for p in range(8 // GROUP):
            q_parts, g_parts, o_parts = [], [], []
            for n in range(GROUP):
                lanes = slice((GROUP * p + n) * DH, (GROUP * p + n + 1) * DH)
                q_parts.append(qbuf[b, :, lanes])
                g_parts += [gbuf[j0, :, lanes], gbuf[j1, :, lanes]]
                o_parts += [att[2 * b, :, lanes], att[2 * b + 1, :, lanes]]
            q2 = jnp.concatenate(q_parts, axis=0)
            g2 = jnp.concatenate(g_parts, axis=0)
            o2 = jnp.concatenate(o_parts, axis=0)
            delta = jnp.sum(g2.astype(jnp.float32) * o2.astype(jnp.float32), axis=1, keepdims=True)
            dprob = lax.dot_general(g2, vwin, dims_nt, preferred_element_type=jnp.float32)
            w = pst[b, p]
            ds = (w.astype(jnp.float32) * (dprob - delta)).astype(jnp.bfloat16)
            dq = (jnp.dot(ds, kwin, preferred_element_type=jnp.float32) * ROOT).astype(jnp.bfloat16)
            dk_sum += lax.dot_general(ds, q2, dims_tn, preferred_element_type=jnp.float32)
            dv_sum += lax.dot_general(w, g2, dims_tn, preferred_element_type=jnp.float32)
            for n in range(GROUP):
                lanes = slice((GROUP * p + n) * DH, (GROUP * p + n + 1) * DH)
                dqs[b, :, lanes] = dq[n * BLK : (n + 1) * BLK]
        dk[rows, :] += dk_sum
        dv[rows, :] += dv_sum

    def pass_att(s):
        m = relayed(s)
        landed(arel.at[m], r_arel.at[m])
        start(copy_af(s))

    loop(8, backward)
    loop(8, pass_att)
    loop(8, lambda b: start(copy_qg(b)))

    start(copy_hal_k)
    start(copy_hal_v)

    def finish(b, k_more=0.0, v_more=0.0):
        rows = al(b + 2, BLK)
        back_turned = jnp.dot(
            (dk[rows, :] + k_more) * ROOT,
            sign[...],
            precision=lax.Precision.HIGHEST,
            preferred_element_type=jnp.float32,
        )
        kst[b] = (back_turned * ROOT).astype(jnp.bfloat16)
        vst[b] = (dv[rows, :] + v_more).astype(jnp.bfloat16)

    loop(6, finish)
    landed(hk, r_hal.at[0])
    landed(hv, r_hal.at[1])
    loop(2, lambda n: finish(n + 6, hk[al(n, BLK), :], hv[al(n, BLK), :]))

    def send_kvg(b):
        start(copy_kg(b))
        start(copy_vg(b))

    loop(8, send_kvg)

    def drain_kv(s):
        drain(copy_k(s))
        drain(copy_v(s))

    def drain_edge(s):
        drain(copy_hk(s))
        drain(copy_hv(s))

    loop(8, drain_kv)

    @pl.when(h >= 6)
    def _():
        loop(8, drain_edge)

    loop(3, lambda s: drain(copy_qr(s)))
    drain(copy_qo())
    loop(4, lambda s: drain(copy_qa(s)))
    loop(3, lambda s: drain(copy_qf(s)))
    loop(16, lambda s: drain(copy_g(s)))

    @pl.when(co == 0)
    def _():
        loop(16, lambda s: drain(copy_att_far(s)))

    @pl.when(co == 1)
    def _():
        loop(16, lambda s: drain(copy_att_near(s)))

    loop(8, lambda s: drain(copy_af(s)))
    loop(8, lambda b: drain(copy_qg(b)))
    loop(8, lambda b: drain(copy_kg(b)))
    loop(8, lambda b: drain(copy_vg(b)))
    drain(copy_hal_k)
    drain(copy_hal_v)
    def due(n):
        landed(qg_o.at[:, al(n, WIDE)], r_qg.at[n])
        landed(kg_o.at[:, al(n, DH)], r_kg.at[n])
        landed(vg_o.at[:, al(n, DH)], r_vg.at[n])

    loop(16, lambda n: landed(att_o.at[al(n // 8, PIECE), al(n % 8, WIDE)], r_att.at[n]))
    loop(8, due)


def copy_kernel(*refs):
    for src, dst in zip(refs[:4], refs[4:]):
        dst[...] = src[...]


def local(queries, keys, values, out_grad, doc_starts, piece_order):
    any_spec = pl.BlockSpec(memory_space=pl.ANY)
    vmem = pl.BlockSpec(memory_space=pltpu.VMEM)
    smem = pl.BlockSpec(memory_space=pltpu.SMEM)
    bf, f32 = jnp.bfloat16, jnp.float32
    shapes = [
        jax.ShapeDtypeStruct(a.shape, bf) for a in (out_grad, queries, keys, values)
    ]
    dma = pltpu.SemaphoreType.DMA
    ext = SHARD + MOST
    results = pl.pallas_call(
        attention_kernel,
        out_shape=shapes,
        in_specs=[any_spec] * 4 + [vmem, smem, vmem],
        out_specs=[any_spec] * 4,
        scratch_shapes=[
            pltpu.VMEM((NHEAD, BLK, WIDE), bf),
            pltpu.VMEM((4, BLK, WIDE), bf),
            pltpu.VMEM((ext, DH), bf),
            pltpu.VMEM((ext, DH), bf),
            pltpu.VMEM((ext, DH), bf),
            pltpu.VMEM((NCTX, PIECE, WIDE), bf),
            pltpu.VMEM((NHEAD, 8 // GROUP, GROUP * BLK, WIN), bf),
            pltpu.VMEM((NCTX, PIECE, WIDE), bf),
            pltpu.VMEM((NCTX, PIECE, WIDE), bf),
            pltpu.VMEM((8, PIECE, WIDE), bf),
            pltpu.VMEM((NHEAD, BLK, WIDE), bf),
            pltpu.VMEM((ext, DH), f32),
            pltpu.VMEM((ext, DH), f32),
            pltpu.VMEM((MOST, DH), f32),
            pltpu.VMEM((MOST, DH), f32),
            pltpu.VMEM((NHEAD, BLK, DH), bf),
            pltpu.VMEM((NHEAD, BLK, DH), bf),
        ]
        + [dma((n,)) for n in (8, 8, 8, 8, 3, 1, 4, 3, 16, 16, 8, 8, 8, 8, 2)]
        + [dma((n,)) for n in (10, 10, 8, 4, 16, 8, 16, 8, 8, 8, 2)],
        compiler_params=pltpu.CompilerParams(
            has_side_effects=True, vmem_limit_bytes=48 * 1024 * 1024
        ),
        name="attention",
    )(
        queries, keys, values, out_grad,
        doc_starts.reshape(1, -1), piece_order, jnp.asarray(sign_grid()),
    )
    blocks = [pl.BlockSpec((PIECE // 4, a.shape[1]), lambda n: (n, 0)) for a in shapes]
    return tuple(
        pl.pallas_call(
            copy_kernel,
            grid=(8,),
            out_shape=shapes,
            in_specs=blocks,
            out_specs=blocks,
            name="place",
        )(*results)
    )


def solution(mesh):
    rows = P(("ctx", "head"), None)
    return jax.shard_map(
        local,
        mesh=mesh,
        in_specs=(rows, rows, rows, rows, P(), P()),
        out_specs=(rows, rows, rows, rows),
        check_vma=False,
    )
```

```python
import functools
import math

import jax
import jax.numpy as jnp
import numpy as np
from jax import lax
from jax.experimental import pallas as pl
from jax.experimental.pallas import tpu as pltpu
from jax.sharding import PartitionSpec as P

MESH = pl.DeviceIdType.MESH
DH = 128
BLK = 128
MOST = 256
WIN = MOST + BLK
PIECE = 64
SHARD = 1024
WIDE = 1024
NCTX = 16
NHEAD = 8
GROUP = 2
NEG = -1e30
ROOT = 1.0 / math.sqrt(DH)


def sign_grid():
    ids = np.arange(DH)
    common = ids[:, None] & ids[None, :]
    parity = np.zeros((DH, DH), np.int64)
    for bit in range(8):
        parity += (common >> bit) & 1
    return np.where(parity % 2 == 0, 1.0, -1.0).astype(np.float32)


def unit(shard, kv):
    even = kv % 2 == 0
    return (
        jnp.where(even, shard, (kv // 2) * 4 + shard % 4),
        jnp.where(even, kv, 2 * (shard // 4) + 1),
    )


def attention_kernel(
    q, k, v, g, docs, order, sign,
    att_o, qg_o, kg_o, vg_o,
    qbuf, qrel, kvin, kvs, kvrel, kvbuf, kraw, kcod, vbuf, gbuf, pst, att, stg, arel, dqs, dk, dv, hk, hv, kst, vst,
    l_kv, s_kvr, s_kvo, s_kva, s_kvf, s_edge, s_qr, s_qo, s_qa, s_qf, s_g, s_att, s_af, s_qg, s_kg, s_vg, s_hal,
    r_kv, r_kvrel, r_q, r_qrel, r_g, r_arel, r_att, r_qg, r_kg, r_vg, r_hal,
):
    c = lax.axis_index("ctx")
    h = lax.axis_index("head")
    z, x, y, co = c // 4, c % 4, h // 2, h % 2
    shard = jnp.where(co == 0, c, y * 4 + x)
    kv = jnp.where(co == 0, 2 * y, 2 * z + 1)

    def al(index, size):
        return pl.ds(pl.multiple_of(index * size, size), size)

    def start(copy):
        src, dst, ssem, rsem, tc, th = copy
        own = (tc == c) & (th == h)

        @pl.when(own)
        def _():
            pltpu.make_async_copy(src, dst, rsem).start()

        @pl.when(jnp.logical_not(own))
        def _():
            pltpu.make_async_remote_copy(
                src, dst, ssem, rsem, device_id={"ctx": tc, "head": th}, device_id_type=MESH
            ).start()

    def drain(copy):
        src, dst, ssem, rsem, tc, th = copy
        own = (tc == c) & (th == h)

        @pl.when(jnp.logical_not(own))
        def _():
            pltpu.make_async_remote_copy(
                src, dst, ssem, rsem, device_id={"ctx": tc, "head": th}, device_id_type=MESH
            ).wait_send()

    def landed(ref, sem):
        pltpu.make_async_copy(ref, ref, sem).wait()

    def loop(count, body):
        def step(s, carry):
            body(s)
            return carry

        lax.fori_loop(0, count, step, 0)

    def far(s):
        return (z + 8 - y - s) % 4

    def copy_kvr(s):
        to = far(s)
        return (kvs.at[2 * to + 1], kvrel.at[z], s_kvr.at[s], r_kvrel.at[z], to * 4 + x, h)

    def copy_kvo():
        return (kvs.at[2 * z + 1], kvbuf.at[h + 2], s_kvo.at[0], r_kv.at[h + 2], c, 2 * z + 1)

    def copy_kva(s):
        to = 2 * ((y + s) % 4)
        return (kvs.at[to], kvbuf.at[h + 2], s_kva.at[s], r_kv.at[h + 2], c, to)

    def copy_kvf(s):
        src = (y + z + s) % 4
        return (kvrel.at[src], kvbuf.at[h + 2], s_kvf.at[s], r_kv.at[h + 2], c, 2 * src + 1)

    def copy_edge(s):
        kk = (h + s) % NHEAD
        return (kvs.at[kk], kvbuf.at[h % 2], s_edge.at[s], r_kv.at[h % 2]) + unit((c + 1) % NCTX, kk)

    def copy_qr(s):
        to = far(s)
        return (q.at[:, al(2 * to + 1, WIDE)], qrel.at[z], s_qr.at[s], r_qrel.at[z], to * 4 + x, h)

    def copy_qo():
        return (q.at[:, al(2 * z + 1, WIDE)], qbuf.at[h], s_qo.at[0], r_q.at[h], c, 2 * z + 1)

    def copy_qa(s):
        to = 2 * ((y + s) % 4)
        return (q.at[:, al(to, WIDE)], qbuf.at[h], s_qa.at[s], r_q.at[h], c, to)

    def copy_qf(s):
        src = (y + z + s) % 4
        return (qrel.at[src], qbuf.at[h], s_qf.at[s], r_q.at[h], c, 2 * src + 1)

    def copy_g(s):
        half = (s // 2 + x) % 2
        step = s // 4
        kk = jnp.where(s % 2 == 0, 2 * ((y + z + step) % 4), 2 * ((z + step) % 4) + 1)
        src = g.at[al(half, PIECE), al(kk, WIDE)]
        return (src, gbuf.at[c], s_g.at[s], r_g.at[c]) + unit(2 * h + half, kk)

    def copy_att_far(s):
        j = (z + 8 - y - s // 4) % 4 * 4 + (x + s) % 4
        slot = z * 2 + x % 2
        return (stg.at[j], arel.at[slot], s_att.at[s], r_arel.at[slot], j, 2 * y + x // 2)

    def copy_att_near(s):
        j = (z + s // 4) % 4 * 4 + (x + s) % 4
        dst = att_o.at[al(x % 2, PIECE), al(kv, WIDE)]
        return (stg.at[j], dst, s_att.at[s], r_att.at[(x % 2) * 8 + kv], j, 2 * y + x // 2)

    def relayed(s):
        return ((y + z + s // 2) % 4) * 2 + s % 2

    def copy_af(s):
        m = relayed(s)
        dst = att_o.at[al(m % 2, PIECE), al(2 * y, WIDE)]
        return (arel.at[m], dst, s_af.at[s], r_att.at[(m % 2) * 8 + 2 * y], c, 2 * (m // 2) + co)

    def copy_qg(b):
        return (dqs.at[b], qg_o.at[:, al(kv, WIDE)], s_qg.at[b], r_qg.at[kv], shard, b)

    def copy_kg(b):
        return (kst.at[b], kg_o.at[:, al(kv, DH)], s_kg.at[b], r_kg.at[kv], shard, b)

    def copy_vg(b):
        return (vst.at[b], vg_o.at[:, al(kv, DH)], s_vg.at[b], r_vg.at[kv], shard, b)

    back = unit((shard + NCTX - 1) % NCTX, kv)
    copy_hal_k = (dk.at[pl.ds(0, MOST)], hk, s_hal.at[0], r_hal.at[0]) + back
    copy_hal_v = (dv.at[pl.ds(0, MOST)], hv, s_hal.at[1], r_hal.at[1]) + back

    load_k = pltpu.make_async_copy(k, kvin.at[0], l_kv.at[0])
    load_v = pltpu.make_async_copy(v, kvin.at[1], l_kv.at[1])
    load_k.start()
    load_v.start()

    def away(s, act, copy):
        @pl.when(far(s) != z)
        def _():
            act(copy(s))

    def others(s, act, copy):
        @pl.when((y + z + s) % 4 != z)
        def _():
            act(copy(s))

    loop(4, lambda s: away(s, start, copy_qr))
    loop(4, lambda s: start(copy_qa(s)))
    start(copy_qo())
    load_k.wait()
    load_v.wait()
    for n in range(NHEAD):
        kvs[n, 0] = kvin[0, :, n * DH : (n + 1) * DH]
        kvs[n, 1] = kvin[1, :, n * DH : (n + 1) * DH]
    loop(4, lambda s: away(s, start, copy_kvr))
    loop(4, lambda s: start(copy_kva(s)))
    start(copy_kvo())

    @pl.when(h >= 6)
    def _():
        loop(8, lambda s: start(copy_edge(s)))

    def pass_on(s):
        src = (y + z + s) % 4

        @pl.when(src != z)
        def _():
            landed(qrel.at[src], r_qrel.at[src])
            start(copy_qf(s))
            landed(kvrel.at[src], r_kvrel.at[src])
            start(copy_kvf(s))

    loop(4, pass_on)
    loop(16, lambda s: start(copy_g(s)))

    dk[...] = jnp.zeros_like(dk)
    dv[...] = jnp.zeros_like(dv)
    starts = docs[...].astype(jnp.float32)

    loop(10, lambda n: landed(kvbuf.at[n], r_kv.at[n]))
    for n in range(10):
        kraw[n * BLK : (n + 1) * BLK] = kvbuf[n, 0]
        vbuf[n * BLK : (n + 1) * BLK] = kvbuf[n, 1]
    turned = jnp.dot(kraw[...], sign[...].astype(jnp.bfloat16), preferred_element_type=jnp.float32)
    kcod[...] = (turned * ROOT).astype(jnp.bfloat16)

    def pair(block, p):
        parts = [block[:, (GROUP * p + n) * DH : (GROUP * p + n + 1) * DH] for n in range(GROUP)]
        return jnp.concatenate(parts, axis=0)

    dims_nt = (((1,), (1,)), ((), ()))
    dims_tn = (((0,), (0,)), ((), ()))

    def forward(s):
        b = (h + 8 - s) % NHEAD
        row = lax.broadcasted_iota(jnp.int32, (BLK, 1), 0) + (shard * SHARD + b * BLK)
        rowf = row.astype(jnp.float32)
        begin = jnp.max(jnp.where(starts <= rowf, starts, 0.0), axis=1, keepdims=True)
        col = lax.broadcasted_iota(jnp.int32, (BLK, WIN), 1) + (shard * SHARD + b * BLK - MOST)
        colf = col.astype(jnp.float32)
        bias = jnp.where((colf <= rowf) & (colf >= begin), 0.0, NEG)
        bias = jnp.concatenate([bias] * GROUP, axis=0)
        kwin = kcod[pl.ds(pl.multiple_of(b * BLK, BLK), WIN), :]
        vwin = vbuf[pl.ds(pl.multiple_of(b * BLK, BLK), WIN), :]
        for p in range(8 // GROUP):
            q2 = jnp.concatenate(
                [qbuf[b, :, (GROUP * p + n) * DH : (GROUP * p + n + 1) * DH] for n in range(GROUP)], axis=0
            )
            score = lax.dot_general(q2, kwin, dims_nt, preferred_element_type=jnp.float32)
            score = score * (ROOT * math.log2(math.e)) + bias
            top = jnp.max(score, axis=1, keepdims=True)
            e = jnp.exp2(score - top)
            total = jnp.sum(e, axis=1, keepdims=True)
            w = (e * (1.0 / total)).astype(jnp.bfloat16)
            pst[b, p] = w
            out = jnp.dot(w, vwin, preferred_element_type=jnp.float32).astype(jnp.bfloat16)
            for n in range(GROUP):
                lanes = slice((GROUP * p + n) * DH, (GROUP * p + n + 1) * DH)
                att[2 * b, :, lanes] = out[n * BLK : n * BLK + PIECE]
                att[2 * b + 1, :, lanes] = out[n * BLK + PIECE : (n + 1) * BLK]

    loop(8, lambda b: landed(qbuf.at[b], r_q.at[b]))
    loop(8, forward)

    def fill(j):
        stg[j] = att[order[shard, j]]

    loop(16, fill)

    def send_att(s):
        @pl.when(co == 0)
        def _():
            start(copy_att_far(s))

        @pl.when(co == 1)
        def _():
            start(copy_att_near(s))

    loop(16, send_att)
    loop(16, lambda j: landed(gbuf.at[j], r_g.at[j]))

    def where_from(piece):
        def look(j, found):
            return jnp.where(order[shard, j] == piece, j, found)

        return lax.fori_loop(0, NCTX, look, 0)

    def backward(s):
        b = (2 * (y + z) + s) % NHEAD
        j0 = where_from(2 * b)
        j1 = where_from(2 * b + 1)
        rows = pl.ds(pl.multiple_of(b * BLK, BLK), WIN)
        kwin = kraw[rows, :]
        vwin = vbuf[rows, :]
        dk_sum = jnp.zeros((WIN, DH), jnp.float32)
        dv_sum = jnp.zeros((WIN, DH), jnp.float32)
        for p in range(8 // GROUP):
            q_parts, g_parts, o_parts = [], [], []
            for n in range(GROUP):
                lanes = slice((GROUP * p + n) * DH, (GROUP * p + n + 1) * DH)
                q_parts.append(qbuf[b, :, lanes])
                g_parts += [gbuf[j0, :, lanes], gbuf[j1, :, lanes]]
                o_parts += [att[2 * b, :, lanes], att[2 * b + 1, :, lanes]]
            q2 = jnp.concatenate(q_parts, axis=0)
            g2 = jnp.concatenate(g_parts, axis=0)
            o2 = jnp.concatenate(o_parts, axis=0)
            delta = jnp.sum(g2.astype(jnp.float32) * o2.astype(jnp.float32), axis=1, keepdims=True)
            dprob = lax.dot_general(g2, vwin, dims_nt, preferred_element_type=jnp.float32)
            w = pst[b, p]
            ds = (w.astype(jnp.float32) * (dprob - delta)).astype(jnp.bfloat16)
            dq = (jnp.dot(ds, kwin, preferred_element_type=jnp.float32) * ROOT).astype(jnp.bfloat16)
            dk_sum += lax.dot_general(ds, q2, dims_tn, preferred_element_type=jnp.float32)
            dv_sum += lax.dot_general(w, g2, dims_tn, preferred_element_type=jnp.float32)
            for n in range(GROUP):
                lanes = slice((GROUP * p + n) * DH, (GROUP * p + n + 1) * DH)
                dqs[b, :, lanes] = dq[n * BLK : (n + 1) * BLK]
        dk[rows, :] += dk_sum
        dv[rows, :] += dv_sum
        start(copy_qg(b))

    def pass_att(s):
        m = relayed(s)
        landed(arel.at[m], r_arel.at[m])
        start(copy_af(s))

    loop(4, backward)
    loop(4, pass_att)
    loop(4, lambda n: backward(n + 4))
    loop(4, lambda n: pass_att(n + 4))

    start(copy_hal_k)
    start(copy_hal_v)

    def finish(b, k_more=0.0, v_more=0.0):
        rows = al(b + 2, BLK)
        back_turned = jnp.dot(
            (dk[rows, :] + k_more) * ROOT,
            sign[...],
            precision=lax.Precision.HIGHEST,
            preferred_element_type=jnp.float32,
        )
        kst[b] = (back_turned * ROOT).astype(jnp.bfloat16)
        vst[b] = (dv[rows, :] + v_more).astype(jnp.bfloat16)

    loop(6, finish)
    landed(hk, r_hal.at[0])
    landed(hv, r_hal.at[1])
    loop(2, lambda n: finish(n + 6, hk[al(n, BLK), :], hv[al(n, BLK), :]))

    def send_kvg(b):
        start(copy_kg(b))
        start(copy_vg(b))

    loop(8, lambda s: send_kvg((2 * (y + z) + s) % NHEAD))

    loop(4, lambda s: away(s, drain, copy_kvr))
    drain(copy_kvo())
    loop(4, lambda s: drain(copy_kva(s)))
    loop(4, lambda s: others(s, drain, copy_kvf))

    @pl.when(h >= 6)
    def _():
        loop(8, lambda s: drain(copy_edge(s)))

    loop(4, lambda s: away(s, drain, copy_qr))
    drain(copy_qo())
    loop(4, lambda s: drain(copy_qa(s)))
    loop(4, lambda s: others(s, drain, copy_qf))
    loop(16, lambda s: drain(copy_g(s)))

    @pl.when(co == 0)
    def _():
        loop(16, lambda s: drain(copy_att_far(s)))

    @pl.when(co == 1)
    def _():
        loop(16, lambda s: drain(copy_att_near(s)))

    loop(8, lambda s: drain(copy_af(s)))
    loop(8, lambda b: drain(copy_qg(b)))
    loop(8, lambda b: drain(copy_kg(b)))
    loop(8, lambda b: drain(copy_vg(b)))
    drain(copy_hal_k)
    drain(copy_hal_v)
    def due(n):
        landed(qg_o.at[:, al(n, WIDE)], r_qg.at[n])
        landed(kg_o.at[:, al(n, DH)], r_kg.at[n])
        landed(vg_o.at[:, al(n, DH)], r_vg.at[n])

    loop(16, lambda n: landed(att_o.at[al(n // 8, PIECE), al(n % 8, WIDE)], r_att.at[n]))
    loop(8, due)


def copy_kernel(*refs):
    sems = refs[-1]
    copies = []
    for n in range(4):
        for part in range(4):
            rows = pl.ds(part * (BLK // 4), BLK // 4)
            copies.append(pltpu.make_async_copy(refs[n].at[rows], refs[4 + n].at[rows], sems.at[n, part]))
    for copy in copies:
        copy.start()
    for copy in copies:
        copy.wait()


def local(queries, keys, values, out_grad, doc_starts, piece_order):
    any_spec = pl.BlockSpec(memory_space=pl.ANY)
    vmem = pl.BlockSpec(memory_space=pltpu.VMEM)
    smem = pl.BlockSpec(memory_space=pltpu.SMEM)
    bf, f32 = jnp.bfloat16, jnp.float32
    shapes = [
        jax.ShapeDtypeStruct(a.shape, bf) for a in (out_grad, queries, keys, values)
    ]
    dma = pltpu.SemaphoreType.DMA
    ext = SHARD + MOST
    results = pl.pallas_call(
        attention_kernel,
        out_shape=shapes,
        in_specs=[any_spec] * 4 + [vmem, smem, vmem],
        out_specs=[any_spec] * 4,
        scratch_shapes=[
            pltpu.VMEM((NHEAD, BLK, WIDE), bf),
            pltpu.VMEM((4, BLK, WIDE), bf),
            pltpu.VMEM((2, BLK, NHEAD * DH), bf),
            pltpu.VMEM((NHEAD, 2, BLK, DH), bf),
            pltpu.VMEM((4, 2, BLK, DH), bf),
            pltpu.VMEM((10, 2, BLK, DH), bf),
            pltpu.VMEM((ext, DH), bf),
            pltpu.VMEM((ext, DH), bf),
            pltpu.VMEM((ext, DH), bf),
            pltpu.VMEM((NCTX, PIECE, WIDE), bf),
            pltpu.VMEM((NHEAD, 8 // GROUP, GROUP * BLK, WIN), bf),
            pltpu.VMEM((NCTX, PIECE, WIDE), bf),
            pltpu.VMEM((NCTX, PIECE, WIDE), bf),
            pltpu.VMEM((8, PIECE, WIDE), bf),
            pltpu.VMEM((NHEAD, BLK, WIDE), bf),
            pltpu.VMEM((ext, DH), f32),
            pltpu.VMEM((ext, DH), f32),
            pltpu.VMEM((MOST, DH), f32),
            pltpu.VMEM((MOST, DH), f32),
            pltpu.VMEM((NHEAD, BLK, DH), bf),
            pltpu.VMEM((NHEAD, BLK, DH), bf),
        ]
        + [dma((n,)) for n in (2, 4, 1, 4, 4, 8, 4, 1, 4, 4, 16, 16, 8, 8, 8, 8, 2)]
        + [dma((n,)) for n in (10, 4, 8, 4, 16, 8, 16, 8, 8, 8, 2)],
        compiler_params=pltpu.CompilerParams(
            has_side_effects=True, vmem_limit_bytes=48 * 1024 * 1024
        ),
        name="attention",
    )(
        queries, keys, values, out_grad,
        doc_starts.reshape(1, -1), piece_order, jnp.asarray(sign_grid()),
    )
    return tuple(
        pl.pallas_call(
            copy_kernel,
            out_shape=shapes,
            in_specs=[vmem] * 4,
            out_specs=[any_spec] * 4,
            scratch_shapes=[dma((4, 4))],
            name="place",
        )(*results)
    )


def solution(mesh):
    rows = P(("ctx", "head"), None)
    return jax.shard_map(
        local,
        mesh=mesh,
        in_specs=(rows, rows, rows, rows, P(), P()),
        out_specs=(rows, rows, rows, rows),
        check_vma=False,
    )
```

```python
import functools
import math

import jax
import jax.numpy as jnp
from jax import lax
from jax.experimental import pallas as pl
from jax.experimental.pallas import tpu as pltpu
from jax.sharding import PartitionSpec as P

MESH = pl.DeviceIdType.MESH
DH = 128
BLK = 128
MOST = 256
WIN = MOST + BLK
PIECE = 64
SHARD = 1024
WIDE = 1024
NCTX = 16
NHEAD = 8
GROUP = 4
NEG = -1e30
MOVES = (
    (1, 1), (3, 3), (1, 3), (3, 1), (1, 0), (3, 0), (0, 1), (0, 3),
    (2, 1), (2, 3), (1, 2), (3, 2), (2, 2), (2, 0), (0, 2), (0, 0),
)
ROOT = 1.0 / math.sqrt(DH)


def sign_grid():
    common = lax.broadcasted_iota(jnp.int32, (DH, DH), 0) & lax.broadcasted_iota(jnp.int32, (DH, DH), 1)
    for shift in (4, 2, 1):
        common = common ^ (common >> shift)
    return (1 - 2 * (common & 1)).astype(jnp.float32)


def unit(shard, kv):
    even = kv % 2 == 0
    return (
        jnp.where(even, shard, (kv // 2) * 4 + shard % 4),
        jnp.where(even, kv, 2 * (shard // 4) + 1),
    )


def attention_kernel(
    q, k, v, g, docs, order,
    att_o, qg_o, kg_o, vg_o,
    qbuf, qrel, kvin, kvs, kvrel, kvbuf, kraw, kcod, vbuf, gbuf, pst, inv, att, stg, arel, dqs, dk, dv, hk, hv, kst, vst,
    l_kv, s_kvr, s_kvo, s_kva, s_kvf, s_edge, s_qr, s_qo, s_qa, s_qf, s_g, s_att, s_af, s_qg, s_kg, s_vg, s_hal,
    r_kv, r_kvrel, r_q, r_qrel, r_g, r_arel, r_att, r_qg, r_kg, r_vg, r_hal,
):
    c = lax.axis_index("ctx")
    h = lax.axis_index("head")
    z, x, y, co = c // 4, c % 4, h // 2, h % 2
    shard = jnp.where(co == 0, c, y * 4 + x)
    kv = jnp.where(co == 0, 2 * y, 2 * z + 1)

    def al(index, size):
        return pl.ds(pl.multiple_of(index * size, size), size)

    def start(copy):
        src, dst, ssem, rsem, tc, th = copy
        own = (tc == c) & (th == h)

        @pl.when(own)
        def _():
            pltpu.make_async_copy(src, dst, rsem).start()

        @pl.when(jnp.logical_not(own))
        def _():
            pltpu.make_async_remote_copy(
                src, dst, ssem, rsem, device_id={"ctx": tc, "head": th}, device_id_type=MESH
            ).start()

    def drain(copy):
        src, dst, ssem, rsem, tc, th = copy
        own = (tc == c) & (th == h)

        @pl.when(jnp.logical_not(own))
        def _():
            pltpu.make_async_remote_copy(
                src, dst, ssem, rsem, device_id={"ctx": tc, "head": th}, device_id_type=MESH
            ).wait_send()

    def landed(ref, sem):
        pltpu.make_async_copy(ref, ref, sem).wait()

    def loop(count, body):
        def step(s, carry):
            body(s)
            return carry

        lax.fori_loop(0, count, step, 0)

    def turn(s):
        return jnp.where(s < 2, 1 + 2 * s, 6 - 2 * s)

    def turn_half(s):
        return jnp.where(s < 4, 1 + 2 * (s % 2), 2 - 2 * (s % 2)), s // 2 % 2

    def far(s):
        return (z + 8 - y - turn(s)) % 4

    def near(s):
        return (y + z + turn(s)) % 4

    def copy_kvr(s):
        to = far(s)
        return (kvs.at[2 * to + 1], kvrel.at[z], s_kvr.at[s], r_kvrel.at[z], to * 4 + x, h)

    def copy_kvo():
        return (kvs.at[2 * z + 1], kvbuf.at[h + 2], s_kvo.at[0], r_kv.at[h + 2], c, 2 * z + 1)

    def copy_kva(s):
        to = 2 * ((y + turn(s)) % 4)
        return (kvs.at[to], kvbuf.at[h + 2], s_kva.at[s], r_kv.at[h + 2], c, to)

    def copy_kvf(s):
        src = near(s)
        return (kvrel.at[src], kvbuf.at[h + 2], s_kvf.at[s], r_kv.at[h + 2], c, 2 * src + 1)

    def copy_edge(s):
        kk = (h + s) % NHEAD
        return (kvs.at[kk], kvbuf.at[h % 2], s_edge.at[s], r_kv.at[h % 2]) + unit((c + 1) % NCTX, kk)

    def copy_qr(s):
        to = far(s)
        return (q.at[:, al(2 * to + 1, WIDE)], qrel.at[z], s_qr.at[s], r_qrel.at[z], to * 4 + x, h)

    def copy_qo():
        return (q.at[:, al(2 * z + 1, WIDE)], qbuf.at[h], s_qo.at[0], r_q.at[h], c, 2 * z + 1)

    def copy_qa(s):
        to = 2 * ((y + turn(s)) % 4)
        return (q.at[:, al(to, WIDE)], qbuf.at[h], s_qa.at[s], r_q.at[h], c, to)

    def copy_qf(s):
        src = near(s)
        return (qrel.at[src], qbuf.at[h], s_qf.at[s], r_q.at[h], c, 2 * src + 1)

    def copy_g(s):
        step, half = turn_half(s % 8)
        half = (half + x) % 2
        kk = jnp.where(s >= 8, 2 * ((y + z + step) % 4), 2 * ((z + step) % 4) + 1)
        src = g.at[al(half, PIECE), al(kk, WIDE)]
        return (src, gbuf.at[c], s_g.at[s], r_g.at[c]) + unit(2 * h + half, kk)

    def copy_att_far(s):
        j = (z + 8 - y - MOVES[s][0]) % 4 * 4 + (x + MOVES[s][1]) % 4
        slot = z * 2 + x % 2
        return (stg.at[j], arel.at[slot], s_att.at[s], r_arel.at[slot], j, 2 * y + x // 2)

    def copy_att_near(s):
        j = (z + MOVES[s][0]) % 4 * 4 + (x + MOVES[s][1]) % 4
        dst = att_o.at[al(x % 2, PIECE), al(kv, WIDE)]
        return (stg.at[j], dst, s_att.at[s], r_att.at[(x % 2) * 8 + kv], j, 2 * y + x // 2)

    def relayed(s):
        step, half = turn_half(s)
        step = jnp.where(s < 4, step, 2 - step)
        return ((y + z + step) % 4) * 2 + half

    def copy_af(s):
        m = relayed(s)
        dst = att_o.at[al(m % 2, PIECE), al(2 * y, WIDE)]
        return (arel.at[m], dst, s_af.at[s], r_att.at[(m % 2) * 8 + 2 * y], c, 2 * (m // 2) + co)

    def copy_qg(b):
        return (dqs.at[b], qg_o.at[:, al(kv, WIDE)], s_qg.at[b], r_qg.at[kv], shard, b)

    def copy_kg(b):
        return (kst.at[b], kg_o.at[:, al(kv, DH)], s_kg.at[b], r_kg.at[kv], shard, b)

    def copy_vg(b):
        return (vst.at[b], vg_o.at[:, al(kv, DH)], s_vg.at[b], r_vg.at[kv], shard, b)

    back = unit((shard + NCTX - 1) % NCTX, kv)
    copy_hal_k = (dk.at[pl.ds(0, MOST)], hk, s_hal.at[0], r_hal.at[0]) + back
    copy_hal_v = (dv.at[pl.ds(0, MOST)], hv, s_hal.at[1], r_hal.at[1]) + back

    load_k = pltpu.make_async_copy(k, kvin.at[0], l_kv.at[0])
    load_v = pltpu.make_async_copy(v, kvin.at[1], l_kv.at[1])
    load_k.start()
    load_v.start()

    def away(s, act, copy):
        @pl.when(far(s) != z)
        def _():
            act(copy(s))

    def others(s, act, copy):
        @pl.when(near(s) != z)
        def _():
            act(copy(s))

    loop(4, lambda s: away(s, start, copy_qr))
    loop(4, lambda s: start(copy_qa(s)))
    start(copy_qo())
    load_k.wait()
    load_v.wait()
    for n in range(NHEAD):
        kvs[n, 0] = kvin[0, :, n * DH : (n + 1) * DH]
        kvs[n, 1] = kvin[1, :, n * DH : (n + 1) * DH]
    loop(4, lambda s: away(s, start, copy_kvr))
    loop(4, lambda s: start(copy_kva(s)))
    start(copy_kvo())

    @pl.when(h >= 6)
    def _():
        loop(8, lambda s: start(copy_edge(s)))

    def pass_on(s):
        src = near(s)

        @pl.when(src != z)
        def _():
            landed(qrel.at[src], r_qrel.at[src])
            start(copy_qf(s))
            landed(kvrel.at[src], r_kvrel.at[src])
            start(copy_kvf(s))

    loop(4, pass_on)
    loop(16, lambda s: start(copy_g(s)))

    dk[...] = jnp.zeros_like(dk)
    dv[...] = jnp.zeros_like(dv)
    starts = docs[...].astype(jnp.float32)

    loop(10, lambda n: landed(kvbuf.at[n], r_kv.at[n]))
    for n in range(10):
        kraw[n * BLK : (n + 1) * BLK] = kvbuf[n, 0]
        vbuf[n * BLK : (n + 1) * BLK, :DH] = kvbuf[n, 1]
    vbuf[:, DH:] = jnp.ones_like(vbuf[:, DH:])
    turned = jnp.dot(kraw[...], sign_grid().astype(jnp.bfloat16), preferred_element_type=jnp.float32)
    kcod[...] = (turned * ROOT).astype(jnp.bfloat16)

    def pair(block, p):
        parts = [block[:, (GROUP * p + n) * DH : (GROUP * p + n + 1) * DH] for n in range(GROUP)]
        return jnp.concatenate(parts, axis=0)

    dims_nt = (((1,), (1,)), ((), ()))
    dims_tn = (((0,), (0,)), ((), ()))

    def forward(s):
        b = (h + 8 - s) % NHEAD
        row = lax.broadcasted_iota(jnp.int32, (BLK, 1), 0) + (shard * SHARD + b * BLK)
        rowf = row.astype(jnp.float32)
        begin = jnp.max(jnp.where(starts <= rowf, starts, 0.0), axis=1, keepdims=True)
        col = lax.broadcasted_iota(jnp.int32, (BLK, WIN), 1) + (shard * SHARD + b * BLK - MOST)
        colf = col.astype(jnp.float32)
        bias = jnp.where((colf <= rowf) & (colf >= begin), 0.0, NEG)
        bias = jnp.concatenate([bias] * GROUP, axis=0)
        kwin = kcod[pl.ds(pl.multiple_of(b * BLK, BLK), WIN), :]
        vwin = vbuf[pl.ds(pl.multiple_of(b * BLK, BLK), WIN), :]
        for p in range(8 // GROUP):
            q2 = jnp.concatenate(
                [qbuf[b, :, (GROUP * p + n) * DH : (GROUP * p + n + 1) * DH] for n in range(GROUP)], axis=0
            )
            score = lax.dot_general(q2, kwin, dims_nt, preferred_element_type=jnp.float32)
            score = score * (ROOT * math.log2(math.e)) + bias
            top = jnp.max(score, axis=1, keepdims=True)
            w = jnp.exp2(score - top).astype(jnp.bfloat16)
            pst[b, p] = w
            both = jnp.dot(w, vwin, preferred_element_type=jnp.float32)
            scale = 1.0 / both[:, DH:]
            inv[b, p] = scale
            out = (both[:, :DH] * scale).astype(jnp.bfloat16)
            for n in range(GROUP):
                lanes = slice((GROUP * p + n) * DH, (GROUP * p + n + 1) * DH)
                att[2 * b, :, lanes] = out[n * BLK : n * BLK + PIECE]
                att[2 * b + 1, :, lanes] = out[n * BLK + PIECE : (n + 1) * BLK]

    loop(8, lambda b: landed(qbuf.at[b], r_q.at[b]))
    loop(8, forward)

    def fill(j):
        stg[j] = att[order[shard, j]]

    loop(16, fill)

    def send_att(s):
        @pl.when(co == 0)
        def _():
            start(copy_att_far(s))

        @pl.when(co == 1)
        def _():
            start(copy_att_near(s))

    for s in range(16):
        send_att(s)
    loop(16, lambda j: landed(gbuf.at[j], r_g.at[j]))

    def where_from(piece):
        def look(j, found):
            return jnp.where(order[shard, j] == piece, j, found)

        return lax.fori_loop(0, NCTX, look, 0)

    def backward(s):
        step, half = turn_half(s)
        b = (2 * (y + z + step) + half) % NHEAD
        j0 = where_from(2 * b)
        j1 = where_from(2 * b + 1)
        rows = pl.ds(pl.multiple_of(b * BLK, BLK), WIN)
        kwin = kraw[rows, :]
        vwin = vbuf[rows, :DH]
        ones = jnp.ones((DH, DH), jnp.bfloat16)
        dk_sum = jnp.zeros((WIN, DH), jnp.float32)
        dv_sum = jnp.zeros((WIN, DH), jnp.float32)
        for p in range(8 // GROUP):
            q_parts, g_parts, o_parts = [], [], []
            for n in range(GROUP):
                lanes = slice((GROUP * p + n) * DH, (GROUP * p + n + 1) * DH)
                q_parts.append(qbuf[b, :, lanes])
                g_parts += [gbuf[j0, :, lanes], gbuf[j1, :, lanes]]
                o_parts += [att[2 * b, :, lanes], att[2 * b + 1, :, lanes]]
            q2 = jnp.concatenate(q_parts, axis=0)
            g2 = jnp.concatenate(g_parts, axis=0)
            o2 = jnp.concatenate(o_parts, axis=0)
            prod = (g2.astype(jnp.float32) * o2.astype(jnp.float32)).astype(jnp.bfloat16)
            delta = jnp.dot(prod, ones, preferred_element_type=jnp.float32)
            dprob = lax.dot_general(g2, vwin, dims_nt, preferred_element_type=jnp.float32)
            w = pst[b, p]
            scale = inv[b, p]
            scaled = jnp.concatenate([scale] * (WIN // DH), axis=1)
            delta = jnp.concatenate([delta] * (WIN // DH), axis=1)
            ds = (w.astype(jnp.float32) * (scaled * (dprob - delta))).astype(jnp.bfloat16)
            g2 = (g2.astype(jnp.float32) * scale).astype(jnp.bfloat16)
            dq = (jnp.dot(ds, kwin, preferred_element_type=jnp.float32) * ROOT).astype(jnp.bfloat16)
            dk_sum += lax.dot_general(ds, q2, dims_tn, preferred_element_type=jnp.float32)
            dv_sum += lax.dot_general(w, g2, dims_tn, preferred_element_type=jnp.float32)
            for n in range(GROUP):
                lanes = slice((GROUP * p + n) * DH, (GROUP * p + n + 1) * DH)
                dqs[b, :, lanes] = dq[n * BLK : (n + 1) * BLK]
        dk[rows, :] += dk_sum
        dv[rows, :] += dv_sum
        start(copy_qg(b))

    def pass_att(s):
        m = relayed(s)
        landed(arel.at[m], r_arel.at[m])
        start(copy_af(s))

    loop(4, pass_att)
    loop(4, backward)
    loop(4, lambda n: pass_att(n + 4))
    loop(4, lambda n: backward(n + 4))

    start(copy_hal_k)
    start(copy_hal_v)

    def finish(b, k_more=0.0, v_more=0.0):
        rows = al(b + 2, BLK)
        back_turned = jnp.dot(
            (dk[rows, :] + k_more) * ROOT,
            sign_grid(),
            precision=lax.Precision.HIGHEST,
            preferred_element_type=jnp.float32,
        )
        kst[b] = (back_turned * ROOT).astype(jnp.bfloat16)
        vst[b] = (dv[rows, :] + v_more).astype(jnp.bfloat16)

    loop(6, finish)
    landed(hk, r_hal.at[0])
    landed(hv, r_hal.at[1])
    loop(2, lambda n: finish(n + 6, hk[al(n, BLK), :], hv[al(n, BLK), :]))

    def send_kvg(b):
        start(copy_kg(b))
        start(copy_vg(b))

    loop(8, lambda s: send_kvg((2 * (y + z) + s) % NHEAD))

    loop(4, lambda s: away(s, drain, copy_kvr))
    drain(copy_kvo())
    loop(4, lambda s: drain(copy_kva(s)))
    loop(4, lambda s: others(s, drain, copy_kvf))

    @pl.when(h >= 6)
    def _():
        loop(8, lambda s: drain(copy_edge(s)))

    loop(4, lambda s: away(s, drain, copy_qr))
    drain(copy_qo())
    loop(4, lambda s: drain(copy_qa(s)))
    loop(4, lambda s: others(s, drain, copy_qf))
    loop(16, lambda s: drain(copy_g(s)))

    @pl.when(co == 0)
    def _():
        for s in range(16):
            drain(copy_att_far(s))

    @pl.when(co == 1)
    def _():
        for s in range(16):
            drain(copy_att_near(s))

    loop(8, lambda s: drain(copy_af(s)))
    loop(8, lambda b: drain(copy_qg(b)))
    loop(8, lambda b: drain(copy_kg(b)))
    loop(8, lambda b: drain(copy_vg(b)))
    drain(copy_hal_k)
    drain(copy_hal_v)
    def due(n):
        landed(qg_o.at[:, al(n, WIDE)], r_qg.at[n])
        landed(kg_o.at[:, al(n, DH)], r_kg.at[n])
        landed(vg_o.at[:, al(n, DH)], r_vg.at[n])

    loop(16, lambda n: landed(att_o.at[al(n // 8, PIECE), al(n % 8, WIDE)], r_att.at[n]))
    loop(8, due)


def local(queries, keys, values, out_grad, doc_starts, piece_order):
    any_spec = pl.BlockSpec(memory_space=pl.ANY)
    vmem = pl.BlockSpec(memory_space=pltpu.VMEM)
    smem = pl.BlockSpec(memory_space=pltpu.SMEM)
    bf, f32 = jnp.bfloat16, jnp.float32
    shapes = [
        jax.ShapeDtypeStruct(a.shape, bf) for a in (out_grad, queries, keys, values)
    ]
    dma = pltpu.SemaphoreType.DMA
    ext = SHARD + MOST
    results = pl.pallas_call(
        attention_kernel,
        out_shape=shapes,
        in_specs=[any_spec] * 4 + [vmem, smem],
        out_specs=[any_spec] * 4,
        scratch_shapes=[
            pltpu.VMEM((NHEAD, BLK, WIDE), bf),
            pltpu.VMEM((4, BLK, WIDE), bf),
            pltpu.VMEM((2, BLK, NHEAD * DH), bf),
            pltpu.VMEM((NHEAD, 2, BLK, DH), bf),
            pltpu.VMEM((4, 2, BLK, DH), bf),
            pltpu.VMEM((10, 2, BLK, DH), bf),
            pltpu.VMEM((ext, DH), bf),
            pltpu.VMEM((ext, DH), bf),
            pltpu.VMEM((ext, 2 * DH), bf),
            pltpu.VMEM((NCTX, PIECE, WIDE), bf),
            pltpu.VMEM((NHEAD, 8 // GROUP, GROUP * BLK, WIN), bf),
            pltpu.VMEM((NHEAD, 8 // GROUP, GROUP * BLK, DH), f32),
            pltpu.VMEM((NCTX, PIECE, WIDE), bf),
            pltpu.VMEM((NCTX, PIECE, WIDE), bf),
            pltpu.VMEM((8, PIECE, WIDE), bf),
            pltpu.VMEM((NHEAD, BLK, WIDE), bf),
            pltpu.VMEM((ext, DH), f32),
            pltpu.VMEM((ext, DH), f32),
            pltpu.VMEM((MOST, DH), f32),
            pltpu.VMEM((MOST, DH), f32),
            pltpu.VMEM((NHEAD, BLK, DH), bf),
            pltpu.VMEM((NHEAD, BLK, DH), bf),
        ]
        + [dma((n,)) for n in (2, 4, 1, 4, 4, 8, 4, 1, 4, 4, 16, 16, 8, 8, 8, 8, 2)]
        + [dma((n,)) for n in (10, 4, 8, 4, 16, 8, 16, 8, 8, 8, 2)],
        compiler_params=pltpu.CompilerParams(
            has_side_effects=True, vmem_limit_bytes=48 * 1024 * 1024
        ),
        name="attention",
    )(
        queries, keys, values, out_grad,
        doc_starts.reshape(1, -1), piece_order,
    )
    return tuple(results)


def solution(mesh):
    rows = P(("ctx", "head"), None)
    return jax.shard_map(
        local,
        mesh=mesh,
        in_specs=(rows, rows, rows, rows, P(), P()),
        out_specs=(rows, rows, rows, rows),
        check_vma=False,
    )
```

```python
import functools
import math

import jax
import jax.numpy as jnp
from jax import lax
from jax.experimental import pallas as pl
from jax.experimental.pallas import tpu as pltpu
from jax.sharding import PartitionSpec as P

MESH = pl.DeviceIdType.MESH
DH = 128
BLK = 128
MOST = 256
WIN = MOST + BLK
PIECE = 64
SHARD = 1024
WIDE = 1024
NCTX = 16
NHEAD = 8
GROUP = 4
NEG = -1e30
MOVES = (
    (1, 1), (3, 3), (1, 3), (3, 1), (1, 0), (3, 0), (0, 1), (0, 3),
    (2, 1), (2, 3), (1, 2), (3, 2), (2, 2), (2, 0), (0, 2), (0, 0),
)
ROOT = 1.0 / math.sqrt(DH)


def sign_grid():
    common = lax.broadcasted_iota(jnp.int32, (DH, DH), 0) & lax.broadcasted_iota(jnp.int32, (DH, DH), 1)
    for shift in (4, 2, 1):
        common = common ^ (common >> shift)
    return (1 - 2 * (common & 1)).astype(jnp.float32)


def unit(shard, kv):
    even = kv % 2 == 0
    return (
        jnp.where(even, shard, (kv // 2) * 4 + shard % 4),
        jnp.where(even, kv, 2 * (shard // 4) + 1),
    )


def attention_kernel(
    q, k, v, g, docs, order,
    att_o, qg_o, kg_o, vg_o,
    qbuf, qrel, kvin, kvs, kvrel, kvbuf, kraw, kcod, vbuf, gbuf, pst, inv, att, stg, arel, dqs, dk, dv, hk, hv, kst, vst,
    l_kv, s_kvr, s_kvo, s_kva, s_kvf, s_edge, s_qr, s_qo, s_qa, s_qf, s_g, s_att, s_af, s_qg, s_kg, s_vg, s_hal,
    r_kv, r_kvrel, r_q, r_qrel, r_g, r_arel, r_att, r_qg, r_kg, r_vg, r_hal,
):
    c = lax.axis_index("ctx")
    h = lax.axis_index("head")
    z, x, y, co = c // 4, c % 4, h // 2, h % 2
    shard = jnp.where(co == 0, c, y * 4 + x)
    kv = jnp.where(co == 0, 2 * y, 2 * z + 1)

    def al(index, size):
        return pl.ds(pl.multiple_of(index * size, size), size)

    def start(copy):
        src, dst, ssem, rsem, tc, th = copy
        own = (tc == c) & (th == h)

        @pl.when(own)
        def _():
            pltpu.make_async_copy(src, dst, rsem).start()

        @pl.when(jnp.logical_not(own))
        def _():
            pltpu.make_async_remote_copy(
                src, dst, ssem, rsem, device_id={"ctx": tc, "head": th}, device_id_type=MESH
            ).start()

    def drain(copy):
        src, dst, ssem, rsem, tc, th = copy
        own = (tc == c) & (th == h)

        @pl.when(jnp.logical_not(own))
        def _():
            pltpu.make_async_remote_copy(
                src, dst, ssem, rsem, device_id={"ctx": tc, "head": th}, device_id_type=MESH
            ).wait_send()

    def landed(ref, sem):
        pltpu.make_async_copy(ref, ref, sem).wait()

    def loop(count, body):
        def step(s, carry):
            body(s)
            return carry

        lax.fori_loop(0, count, step, 0)

    def turn(s):
        return jnp.where(s < 2, 1 + 2 * s, 6 - 2 * s)

    def turn_half(s):
        return jnp.where(s < 4, 1 + 2 * (s % 2), 2 - 2 * (s % 2)), s // 2 % 2

    def far(s):
        return (z + 8 - y - turn(s)) % 4

    def near(s):
        return (y + z + turn(s)) % 4

    def copy_kvr(s):
        to = far(s)
        return (kvs.at[2 * to + 1], kvrel.at[z], s_kvr.at[s], r_kvrel.at[z], to * 4 + x, h)

    def copy_kvo():
        return (kvs.at[2 * z + 1], kvbuf.at[h + 2], s_kvo.at[0], r_kv.at[h + 2], c, 2 * z + 1)

    def copy_kva(s):
        to = 2 * ((y + turn(s)) % 4)
        return (kvs.at[to], kvbuf.at[h + 2], s_kva.at[s], r_kv.at[h + 2], c, to)

    def copy_kvf(s):
        src = near(s)
        return (kvrel.at[src], kvbuf.at[h + 2], s_kvf.at[s], r_kv.at[h + 2], c, 2 * src + 1)

    def copy_edge(s):
        kk = (h + s) % NHEAD
        return (kvs.at[kk], kvbuf.at[h % 2], s_edge.at[s], r_kv.at[h % 2]) + unit((c + 1) % NCTX, kk)

    def copy_qr(s):
        to = far(s)
        return (q.at[:, al(2 * to + 1, WIDE)], qrel.at[z], s_qr.at[s], r_qrel.at[z], to * 4 + x, h)

    def copy_qo():
        return (q.at[:, al(2 * z + 1, WIDE)], qbuf.at[h], s_qo.at[0], r_q.at[h], c, 2 * z + 1)

    def copy_qa(s):
        to = 2 * ((y + turn(s)) % 4)
        return (q.at[:, al(to, WIDE)], qbuf.at[h], s_qa.at[s], r_q.at[h], c, to)

    def copy_qf(s):
        src = near(s)
        return (qrel.at[src], qbuf.at[h], s_qf.at[s], r_q.at[h], c, 2 * src + 1)

    def copy_g(s):
        step, half = turn_half(s % 8)
        half = (half + x) % 2
        kk = jnp.where(s >= 8, 2 * ((y + z + step) % 4), 2 * ((z + step) % 4) + 1)
        src = g.at[al(half, PIECE), al(kk, WIDE)]
        return (src, gbuf.at[c], s_g.at[s], r_g.at[c]) + unit(2 * h + half, kk)

    def copy_att_far(s):
        j = (z + 8 - y - MOVES[s][0]) % 4 * 4 + (x + MOVES[s][1]) % 4
        slot = z * 2 + x % 2
        return (stg.at[j], arel.at[slot], s_att.at[s], r_arel.at[slot], j, 2 * y + x // 2)

    def copy_att_near(s):
        j = (z + MOVES[s][0]) % 4 * 4 + (x + MOVES[s][1]) % 4
        dst = att_o.at[al(x % 2, PIECE), al(kv, WIDE)]
        return (stg.at[j], dst, s_att.at[s], r_att.at[(x % 2) * 8 + kv], j, 2 * y + x // 2)

    def relayed(s):
        step, half = turn_half(s)
        step = jnp.where(s < 4, step, 2 - step)
        return ((y + z + step) % 4) * 2 + half

    def copy_af(s):
        m = relayed(s)
        dst = att_o.at[al(m % 2, PIECE), al(2 * y, WIDE)]
        return (arel.at[m], dst, s_af.at[s], r_att.at[(m % 2) * 8 + 2 * y], c, 2 * (m // 2) + co)

    def copy_qg(b):
        return (dqs.at[b], qg_o.at[:, al(kv, WIDE)], s_qg.at[b], r_qg.at[kv], shard, b)

    def copy_kg(b):
        return (kst.at[b], kg_o.at[:, al(kv, DH)], s_kg.at[b], r_kg.at[kv], shard, b)

    def copy_vg(b):
        return (vst.at[b], vg_o.at[:, al(kv, DH)], s_vg.at[b], r_vg.at[kv], shard, b)

    back = unit((shard + NCTX - 1) % NCTX, kv)
    copy_hal_k = (dk.at[pl.ds(0, MOST)], hk, s_hal.at[0], r_hal.at[0]) + back
    copy_hal_v = (dv.at[pl.ds(0, MOST)], hv, s_hal.at[1], r_hal.at[1]) + back

    barrier = pltpu.get_barrier_semaphore()

    def greet(t):
        pl.semaphore_signal(
            barrier, inc=1, device_id={"ctx": t // NHEAD, "head": t % NHEAD}, device_id_type=MESH
        )

    loop(NCTX * NHEAD, greet)
    pl.semaphore_wait(barrier, NCTX * NHEAD)

    load_k = pltpu.make_async_copy(k, kvin.at[0], l_kv.at[0])
    load_v = pltpu.make_async_copy(v, kvin.at[1], l_kv.at[1])
    load_k.start()
    load_v.start()

    def away(s, act, copy):
        @pl.when(far(s) != z)
        def _():
            act(copy(s))

    def others(s, act, copy):
        @pl.when(near(s) != z)
        def _():
            act(copy(s))

    loop(4, lambda s: away(s, start, copy_qr))
    loop(4, lambda s: start(copy_qa(s)))
    start(copy_qo())
    load_k.wait()
    load_v.wait()
    for n in range(NHEAD):
        kvs[n, 0] = kvin[0, :, n * DH : (n + 1) * DH]
        kvs[n, 1] = kvin[1, :, n * DH : (n + 1) * DH]
    loop(4, lambda s: away(s, start, copy_kvr))
    loop(4, lambda s: start(copy_kva(s)))
    start(copy_kvo())

    @pl.when(h >= 6)
    def _():
        loop(8, lambda s: start(copy_edge(s)))

    def pass_on(s):
        src = near(s)

        @pl.when(src != z)
        def _():
            landed(qrel.at[src], r_qrel.at[src])
            start(copy_qf(s))
            landed(kvrel.at[src], r_kvrel.at[src])
            start(copy_kvf(s))

    loop(4, pass_on)
    loop(16, lambda s: start(copy_g(s)))

    dk[...] = jnp.zeros_like(dk)
    dv[...] = jnp.zeros_like(dv)
    starts = docs[...].astype(jnp.float32)

    loop(10, lambda n: landed(kvbuf.at[n], r_kv.at[n]))
    for n in range(10):
        kraw[n * BLK : (n + 1) * BLK] = kvbuf[n, 0]
        vbuf[n * BLK : (n + 1) * BLK, :DH] = kvbuf[n, 1]
    vbuf[:, DH:] = jnp.ones_like(vbuf[:, DH:])
    turned = jnp.dot(kraw[...], sign_grid().astype(jnp.bfloat16), preferred_element_type=jnp.float32)
    kcod[...] = (turned * ROOT).astype(jnp.bfloat16)

    def pair(block, p):
        parts = [block[:, (GROUP * p + n) * DH : (GROUP * p + n + 1) * DH] for n in range(GROUP)]
        return jnp.concatenate(parts, axis=0)

    dims_nt = (((1,), (1,)), ((), ()))
    dims_tn = (((0,), (0,)), ((), ()))

    def forward(s):
        b = (h + 8 - s) % NHEAD
        row = lax.broadcasted_iota(jnp.int32, (BLK, 1), 0) + (shard * SHARD + b * BLK)
        rowf = row.astype(jnp.float32)
        begin = jnp.max(jnp.where(starts <= rowf, starts, 0.0), axis=1, keepdims=True)
        col = lax.broadcasted_iota(jnp.int32, (BLK, WIN), 1) + (shard * SHARD + b * BLK - MOST)
        colf = col.astype(jnp.float32)
        bias = jnp.where((colf <= rowf) & (colf >= begin), 0.0, NEG)
        bias = jnp.concatenate([bias] * GROUP, axis=0)
        kwin = kcod[pl.ds(pl.multiple_of(b * BLK, BLK), WIN), :]
        vwin = vbuf[pl.ds(pl.multiple_of(b * BLK, BLK), WIN), :]
        for p in range(8 // GROUP):
            q2 = jnp.concatenate(
                [qbuf[b, :, (GROUP * p + n) * DH : (GROUP * p + n + 1) * DH] for n in range(GROUP)], axis=0
            )
            score = lax.dot_general(q2, kwin, dims_nt, preferred_element_type=jnp.float32)
            score = score * (ROOT * math.log2(math.e)) + bias
            top = jnp.max(score, axis=1, keepdims=True)
            w = jnp.exp2(score - top).astype(jnp.bfloat16)
            pst[b, p] = w
            both = jnp.dot(w, vwin, preferred_element_type=jnp.float32)
            scale = 1.0 / both[:, DH:]
            inv[b, p] = scale
            out = (both[:, :DH] * scale).astype(jnp.bfloat16)
            for n in range(GROUP):
                lanes = slice((GROUP * p + n) * DH, (GROUP * p + n + 1) * DH)
                att[2 * b, :, lanes] = out[n * BLK : n * BLK + PIECE]
                att[2 * b + 1, :, lanes] = out[n * BLK + PIECE : (n + 1) * BLK]

    loop(8, lambda b: landed(qbuf.at[b], r_q.at[b]))
    loop(8, forward)

    def fill(j):
        stg[j] = att[order[shard, j]]

    loop(16, fill)

    def send_att(s):
        @pl.when(co == 0)
        def _():
            start(copy_att_far(s))

        @pl.when(co == 1)
        def _():
            start(copy_att_near(s))

    for s in range(16):
        send_att(s)
    loop(16, lambda j: landed(gbuf.at[j], r_g.at[j]))

    def where_from(piece):
        def look(j, found):
            return jnp.where(order[shard, j] == piece, j, found)

        return lax.fori_loop(0, NCTX, look, 0)

    def backward(b):
        j0 = where_from(2 * b)
        j1 = where_from(2 * b + 1)
        rows = pl.ds(pl.multiple_of(b * BLK, BLK), WIN)
        kwin = kraw[rows, :]
        vwin = vbuf[rows, :DH]
        ones = jnp.ones((DH, DH), jnp.bfloat16)
        dk_sum = jnp.zeros((WIN, DH), jnp.float32)
        dv_sum = jnp.zeros((WIN, DH), jnp.float32)
        for p in range(8 // GROUP):
            q_parts, g_parts, o_parts = [], [], []
            for n in range(GROUP):
                lanes = slice((GROUP * p + n) * DH, (GROUP * p + n + 1) * DH)
                q_parts.append(qbuf[b, :, lanes])
                g_parts += [gbuf[j0, :, lanes], gbuf[j1, :, lanes]]
                o_parts += [att[2 * b, :, lanes], att[2 * b + 1, :, lanes]]
            q2 = jnp.concatenate(q_parts, axis=0)
            g2 = jnp.concatenate(g_parts, axis=0)
            o2 = jnp.concatenate(o_parts, axis=0)
            prod = (g2.astype(jnp.float32) * o2.astype(jnp.float32)).astype(jnp.bfloat16)
            delta = jnp.dot(prod, ones, preferred_element_type=jnp.float32)
            dprob = lax.dot_general(g2, vwin, dims_nt, preferred_element_type=jnp.float32)
            w = pst[b, p]
            scale = inv[b, p]
            scaled = jnp.concatenate([scale] * (WIN // DH), axis=1)
            delta = jnp.concatenate([delta] * (WIN // DH), axis=1)
            ds = (w.astype(jnp.float32) * (scaled * (dprob - delta))).astype(jnp.bfloat16)
            g2 = (g2.astype(jnp.float32) * scale).astype(jnp.bfloat16)
            dq = (jnp.dot(ds, kwin, preferred_element_type=jnp.float32) * ROOT).astype(jnp.bfloat16)
            dk_sum += lax.dot_general(ds, q2, dims_tn, preferred_element_type=jnp.float32)
            dv_sum += lax.dot_general(w, g2, dims_tn, preferred_element_type=jnp.float32)
            for n in range(GROUP):
                lanes = slice((GROUP * p + n) * DH, (GROUP * p + n + 1) * DH)
                dqs[b, :, lanes] = dq[n * BLK : (n + 1) * BLK]
        dk[rows, :] += dk_sum
        dv[rows, :] += dv_sum

    def backward_step(s):
        step, half = turn_half(s)
        b = (2 * (y + z + step) + half) % NHEAD

        @pl.when(b >= 2)
        def _():
            backward(b)

        start(copy_qg(b))

    def pass_att(s):
        m = relayed(s)
        landed(arel.at[m], r_arel.at[m])
        start(copy_af(s))

    loop(2, backward)
    start(copy_hal_k)
    start(copy_hal_v)
    loop(2, backward_step)
    loop(4, pass_att)
    loop(2, lambda n: backward_step(n + 2))
    loop(4, lambda n: pass_att(n + 4))
    loop(4, lambda n: backward_step(n + 4))

    def finish(b, k_more=0.0, v_more=0.0):
        rows = al(b + 2, BLK)
        back_turned = jnp.dot(
            (dk[rows, :] + k_more) * ROOT,
            sign_grid(),
            precision=lax.Precision.HIGHEST,
            preferred_element_type=jnp.float32,
        )
        kst[b] = (back_turned * ROOT).astype(jnp.bfloat16)
        vst[b] = (dv[rows, :] + v_more).astype(jnp.bfloat16)

    loop(6, finish)
    landed(hk, r_hal.at[0])
    landed(hv, r_hal.at[1])
    loop(2, lambda n: finish(n + 6, hk[al(n, BLK), :], hv[al(n, BLK), :]))

    def send_kvg(b):
        start(copy_kg(b))
        start(copy_vg(b))

    loop(8, lambda s: send_kvg((2 * (y + z) + s) % NHEAD))

    loop(4, lambda s: away(s, drain, copy_kvr))
    drain(copy_kvo())
    loop(4, lambda s: drain(copy_kva(s)))
    loop(4, lambda s: others(s, drain, copy_kvf))

    @pl.when(h >= 6)
    def _():
        loop(8, lambda s: drain(copy_edge(s)))

    loop(4, lambda s: away(s, drain, copy_qr))
    drain(copy_qo())
    loop(4, lambda s: drain(copy_qa(s)))
    loop(4, lambda s: others(s, drain, copy_qf))
    loop(16, lambda s: drain(copy_g(s)))

    @pl.when(co == 0)
    def _():
        for s in range(16):
            drain(copy_att_far(s))

    @pl.when(co == 1)
    def _():
        for s in range(16):
            drain(copy_att_near(s))

    loop(8, lambda s: drain(copy_af(s)))
    loop(8, lambda b: drain(copy_qg(b)))
    loop(8, lambda b: drain(copy_kg(b)))
    loop(8, lambda b: drain(copy_vg(b)))
    drain(copy_hal_k)
    drain(copy_hal_v)
    def due(n):
        landed(qg_o.at[:, al(n, WIDE)], r_qg.at[n])
        landed(kg_o.at[:, al(n, DH)], r_kg.at[n])
        landed(vg_o.at[:, al(n, DH)], r_vg.at[n])

    loop(16, lambda n: landed(att_o.at[al(n // 8, PIECE), al(n % 8, WIDE)], r_att.at[n]))
    loop(8, due)


def local(queries, keys, values, out_grad, doc_starts, piece_order):
    any_spec = pl.BlockSpec(memory_space=pl.ANY)
    vmem = pl.BlockSpec(memory_space=pltpu.VMEM)
    smem = pl.BlockSpec(memory_space=pltpu.SMEM)
    bf, f32 = jnp.bfloat16, jnp.float32
    shapes = [
        jax.ShapeDtypeStruct(a.shape, bf) for a in (out_grad, queries, keys, values)
    ]
    dma = pltpu.SemaphoreType.DMA
    ext = SHARD + MOST
    results = pl.pallas_call(
        attention_kernel,
        out_shape=shapes,
        in_specs=[any_spec] * 4 + [vmem, smem],
        out_specs=[any_spec] * 4,
        scratch_shapes=[
            pltpu.VMEM((NHEAD, BLK, WIDE), bf),
            pltpu.VMEM((4, BLK, WIDE), bf),
            pltpu.VMEM((2, BLK, NHEAD * DH), bf),
            pltpu.VMEM((NHEAD, 2, BLK, DH), bf),
            pltpu.VMEM((4, 2, BLK, DH), bf),
            pltpu.VMEM((10, 2, BLK, DH), bf),
            pltpu.VMEM((ext, DH), bf),
            pltpu.VMEM((ext, DH), bf),
            pltpu.VMEM((ext, 2 * DH), bf),
            pltpu.VMEM((NCTX, PIECE, WIDE), bf),
            pltpu.VMEM((NHEAD, 8 // GROUP, GROUP * BLK, WIN), bf),
            pltpu.VMEM((NHEAD, 8 // GROUP, GROUP * BLK, DH), f32),
            pltpu.VMEM((NCTX, PIECE, WIDE), bf),
            pltpu.VMEM((NCTX, PIECE, WIDE), bf),
            pltpu.VMEM((8, PIECE, WIDE), bf),
            pltpu.VMEM((NHEAD, BLK, WIDE), bf),
            pltpu.VMEM((ext, DH), f32),
            pltpu.VMEM((ext, DH), f32),
            pltpu.VMEM((MOST, DH), f32),
            pltpu.VMEM((MOST, DH), f32),
            pltpu.VMEM((NHEAD, BLK, DH), bf),
            pltpu.VMEM((NHEAD, BLK, DH), bf),
        ]
        + [dma((n,)) for n in (2, 4, 1, 4, 4, 8, 4, 1, 4, 4, 16, 16, 8, 8, 8, 8, 2)]
        + [dma((n,)) for n in (10, 4, 8, 4, 16, 8, 16, 8, 8, 8, 2)],
        compiler_params=pltpu.CompilerParams(
            collective_id=0, has_side_effects=True, vmem_limit_bytes=48 * 1024 * 1024
        ),
        name="attention",
    )(
        queries, keys, values, out_grad,
        doc_starts.reshape(1, -1), piece_order,
    )
    return tuple(results)


def solution(mesh):
    rows = P(("ctx", "head"), None)
    return jax.shard_map(
        local,
        mesh=mesh,
        in_specs=(rows, rows, rows, rows, P(), P()),
        out_specs=(rows, rows, rows, rows),
        check_vma=False,
    )
```

```python
import functools
import math

import jax
import jax.numpy as jnp
from jax import lax
from jax.experimental import pallas as pl
from jax.experimental.pallas import tpu as pltpu
from jax.sharding import PartitionSpec as P

MESH = pl.DeviceIdType.MESH
DH = 128
BLK = 128
MOST = 256
WIN = MOST + BLK
PIECE = 64
SHARD = 1024
WIDE = 1024
NCTX = 16
NHEAD = 8
GROUP = 4
NEG = -1e30
MOVES = (
    (1, 1), (3, 3), (1, 3), (3, 1), (1, 0), (3, 0), (0, 1), (0, 3),
    (2, 1), (2, 3), (1, 2), (3, 2), (2, 2), (2, 0), (0, 2), (0, 0),
)
ROOT = 1.0 / math.sqrt(DH)


def sign_grid():
    common = lax.broadcasted_iota(jnp.int32, (DH, DH), 0) & lax.broadcasted_iota(jnp.int32, (DH, DH), 1)
    for shift in (4, 2, 1):
        common = common ^ (common >> shift)
    return (1 - 2 * (common & 1)).astype(jnp.float32)


def unit(shard, kv):
    even = kv % 2 == 0
    return (
        jnp.where(even, shard, (kv // 2) * 4 + shard % 4),
        jnp.where(even, kv, 2 * (shard // 4) + 1),
    )


def attention_kernel(
    q, k, v, g, docs, order,
    att_o, qg_o, kg_o, vg_o,
    qbuf, qrel, kvs, kvrel, kvbuf, kraw, kcod, vbuf, gbuf, pst, inv, att, stg, arel, dqs, dk, dv, hk, hv, kvst, kvland,
    s_kvr, s_kvo, s_kva, s_kvf, s_edge, s_qr, s_qo, s_qa, s_qf, s_g, s_att, s_af, s_qg, s_kg, s_hal,
    r_kv, r_kvrel, r_q, r_qrel, r_g, r_arel, r_att, r_qg, r_kg, r_hal,
):
    c = lax.axis_index("ctx")
    h = lax.axis_index("head")
    z, x, y, co = c // 4, c % 4, h // 2, h % 2
    shard = jnp.where(co == 0, c, y * 4 + x)
    kv = jnp.where(co == 0, 2 * y, 2 * z + 1)

    def al(index, size):
        return pl.ds(pl.multiple_of(index * size, size), size)

    def start(copy):
        src, dst, ssem, rsem, tc, th = copy
        own = (tc == c) & (th == h)

        @pl.when(own)
        def _():
            pltpu.make_async_copy(src, dst, rsem).start()

        @pl.when(jnp.logical_not(own))
        def _():
            pltpu.make_async_remote_copy(
                src, dst, ssem, rsem, device_id={"ctx": tc, "head": th}, device_id_type=MESH
            ).start()

    def drain(copy):
        src, dst, ssem, rsem, tc, th = copy
        own = (tc == c) & (th == h)

        @pl.when(jnp.logical_not(own))
        def _():
            pltpu.make_async_remote_copy(
                src, dst, ssem, rsem, device_id={"ctx": tc, "head": th}, device_id_type=MESH
            ).wait_send()

    def landed(ref, sem):
        pltpu.make_async_copy(ref, ref, sem).wait()

    def loop(count, body):
        def step(s, carry):
            body(s)
            return carry

        lax.fori_loop(0, count, step, 0)

    def turn(s):
        return jnp.where(s < 2, 1 + 2 * s, 6 - 2 * s)

    def turn_half(s):
        return jnp.where(s < 4, 1 + 2 * (s % 2), 2 - 2 * (s % 2)), s // 2 % 2

    def far(s):
        return (z + 8 - y - turn(s)) % 4

    def near(s):
        return (y + z + turn(s)) % 4

    def copy_kvr(s):
        to = far(s)
        return (kvs.at[2 * to + 1], kvrel.at[z], s_kvr.at[s], r_kvrel.at[z], to * 4 + x, h)

    def copy_kvo():
        return (kvs.at[2 * z + 1], kvbuf.at[h + 2], s_kvo.at[0], r_kv.at[h + 2], c, 2 * z + 1)

    def copy_kva(s):
        to = 2 * ((y + turn(s)) % 4)
        return (kvs.at[to], kvbuf.at[h + 2], s_kva.at[s], r_kv.at[h + 2], c, to)

    def copy_kvf(s):
        src = near(s)
        return (kvrel.at[src], kvbuf.at[h + 2], s_kvf.at[s], r_kv.at[h + 2], c, 2 * src + 1)

    def copy_edge(s):
        kk = (h + s) % NHEAD
        return (kvs.at[kk], kvbuf.at[h % 2], s_edge.at[s], r_kv.at[h % 2]) + unit((c + 1) % NCTX, kk)

    def copy_qr(s):
        to = far(s)
        return (q.at[:, al(2 * to + 1, WIDE)], qrel.at[z], s_qr.at[s], r_qrel.at[z], to * 4 + x, h)

    def copy_qo():
        return (q.at[:, al(2 * z + 1, WIDE)], qbuf.at[h], s_qo.at[0], r_q.at[h], c, 2 * z + 1)

    def copy_qa(s):
        to = 2 * ((y + turn(s)) % 4)
        return (q.at[:, al(to, WIDE)], qbuf.at[h], s_qa.at[s], r_q.at[h], c, to)

    def copy_qf(s):
        src = near(s)
        return (qrel.at[src], qbuf.at[h], s_qf.at[s], r_q.at[h], c, 2 * src + 1)

    def copy_g(s):
        step, half = turn_half(s % 8)
        half = (half + x) % 2
        kk = jnp.where(s >= 8, 2 * ((y + z + step) % 4), 2 * ((z + step) % 4) + 1)
        src = g.at[al(half, PIECE), al(kk, WIDE)]
        return (src, gbuf.at[c], s_g.at[s], r_g.at[c]) + unit(2 * h + half, kk)

    def copy_att_far(s):
        j = (z + 8 - y - MOVES[s][0]) % 4 * 4 + (x + MOVES[s][1]) % 4
        slot = z * 2 + x % 2
        return (stg.at[j], arel.at[slot], s_att.at[s], r_arel.at[slot], j, 2 * y + x // 2)

    def copy_att_near(s):
        j = (z + MOVES[s][0]) % 4 * 4 + (x + MOVES[s][1]) % 4
        dst = att_o.at[al(x % 2, PIECE), al(kv, WIDE)]
        return (stg.at[j], dst, s_att.at[s], r_att.at[(x % 2) * 8 + kv], j, 2 * y + x // 2)

    def relayed(s):
        step, half = turn_half(s)
        step = jnp.where(s < 4, step, 2 - step)
        return ((y + z + step) % 4) * 2 + half

    def copy_af(s):
        m = relayed(s)
        dst = att_o.at[al(m % 2, PIECE), al(2 * y, WIDE)]
        return (arel.at[m], dst, s_af.at[s], r_att.at[(m % 2) * 8 + 2 * y], c, 2 * (m // 2) + co)

    def copy_qg(b):
        return (dqs.at[b], qg_o.at[:, al(kv, WIDE)], s_qg.at[b], r_qg.at[kv], shard, b)

    def copy_kg(b):
        return (kvst.at[b], kvland.at[kv], s_kg.at[b], r_kg.at[kv], shard, b)

    back = unit((shard + NCTX - 1) % NCTX, kv)
    copy_hal_k = (dk.at[pl.ds(0, MOST)], hk, s_hal.at[0], r_hal.at[0]) + back
    copy_hal_v = (dv.at[pl.ds(0, MOST)], hv, s_hal.at[1], r_hal.at[1]) + back

    barrier = pltpu.get_barrier_semaphore()

    def greet(t):
        pl.semaphore_signal(
            barrier, inc=1, device_id={"ctx": t // NHEAD, "head": t % NHEAD}, device_id_type=MESH
        )

    loop(NCTX * NHEAD, greet)
    for n in range(NHEAD):
        kvs[n, 0] = k[:, n * DH : (n + 1) * DH]
        kvs[n, 1] = v[:, n * DH : (n + 1) * DH]
    dk[...] = jnp.zeros_like(dk)
    dv[...] = jnp.zeros_like(dv)
    vbuf[:, DH:] = jnp.ones_like(vbuf[:, DH:])
    pl.semaphore_wait(barrier, NCTX * NHEAD)

    def away(s, act, copy):
        @pl.when(far(s) != z)
        def _():
            act(copy(s))

    def others(s, act, copy):
        @pl.when(near(s) != z)
        def _():
            act(copy(s))

    loop(4, lambda s: away(s, start, copy_qr))
    loop(4, lambda s: start(copy_qa(s)))
    start(copy_qo())
    loop(4, lambda s: away(s, start, copy_kvr))
    loop(4, lambda s: start(copy_kva(s)))
    start(copy_kvo())

    @pl.when(h >= 6)
    def _():
        loop(8, lambda s: start(copy_edge(s)))

    def pass_on(s):
        src = near(s)

        @pl.when(src != z)
        def _():
            landed(qrel.at[src], r_qrel.at[src])
            start(copy_qf(s))
            landed(kvrel.at[src], r_kvrel.at[src])
            start(copy_kvf(s))

    loop(4, pass_on)
    loop(16, lambda s: start(copy_g(s)))

    starts = docs[...].astype(jnp.float32)

    loop(10, lambda n: landed(kvbuf.at[n], r_kv.at[n]))
    for n in range(10):
        kraw[n * BLK : (n + 1) * BLK] = kvbuf[n, 0]
        vbuf[n * BLK : (n + 1) * BLK, :DH] = kvbuf[n, 1]
    turned = jnp.dot(kraw[...], sign_grid().astype(jnp.bfloat16), preferred_element_type=jnp.float32)
    kcod[...] = (turned * ROOT).astype(jnp.bfloat16)

    def pair(block, p):
        parts = [block[:, (GROUP * p + n) * DH : (GROUP * p + n + 1) * DH] for n in range(GROUP)]
        return jnp.concatenate(parts, axis=0)

    dims_nt = (((1,), (1,)), ((), ()))
    dims_tn = (((0,), (0,)), ((), ()))

    def forward(s):
        b = (h + 8 - s) % NHEAD
        row = lax.broadcasted_iota(jnp.int32, (BLK, 1), 0) + (shard * SHARD + b * BLK)
        rowf = row.astype(jnp.float32)
        begin = jnp.max(jnp.where(starts <= rowf, starts, 0.0), axis=1, keepdims=True)
        col = lax.broadcasted_iota(jnp.int32, (BLK, WIN), 1) + (shard * SHARD + b * BLK - MOST)
        colf = col.astype(jnp.float32)
        bias = jnp.where((colf <= rowf) & (colf >= begin), 0.0, NEG)
        bias = jnp.concatenate([bias] * GROUP, axis=0)
        kwin = kcod[pl.ds(pl.multiple_of(b * BLK, BLK), WIN), :]
        vwin = vbuf[pl.ds(pl.multiple_of(b * BLK, BLK), WIN), :]
        for p in range(8 // GROUP):
            q2 = jnp.concatenate(
                [qbuf[b, :, (GROUP * p + n) * DH : (GROUP * p + n + 1) * DH] for n in range(GROUP)], axis=0
            )
            score = lax.dot_general(q2, kwin, dims_nt, preferred_element_type=jnp.float32)
            score = score * (ROOT * math.log2(math.e)) + bias
            top = jnp.max(score, axis=1, keepdims=True)
            w = jnp.exp2(score - top).astype(jnp.bfloat16)
            pst[b, p] = w
            both = jnp.dot(w, vwin, preferred_element_type=jnp.float32)
            scale = 1.0 / both[:, DH:]
            inv[b, p] = scale
            out = (both[:, :DH] * scale).astype(jnp.bfloat16)
            for n in range(GROUP):
                lanes = slice((GROUP * p + n) * DH, (GROUP * p + n + 1) * DH)
                att[2 * b, :, lanes] = out[n * BLK : n * BLK + PIECE]
                att[2 * b + 1, :, lanes] = out[n * BLK + PIECE : (n + 1) * BLK]

    loop(8, lambda b: landed(qbuf.at[b], r_q.at[b]))
    loop(8, forward)

    def fill(j):
        stg[j] = att[order[shard, j]]

    loop(16, fill)

    def send_att(s):
        @pl.when(co == 0)
        def _():
            start(copy_att_far(s))

        @pl.when(co == 1)
        def _():
            start(copy_att_near(s))

    for s in range(16):
        send_att(s)
    loop(16, lambda j: landed(gbuf.at[j], r_g.at[j]))

    def where_from(piece):
        def look(j, found):
            return jnp.where(order[shard, j] == piece, j, found)

        return lax.fori_loop(0, NCTX, look, 0)

    def backward(b):
        j0 = where_from(2 * b)
        j1 = where_from(2 * b + 1)
        rows = pl.ds(pl.multiple_of(b * BLK, BLK), WIN)
        kwin = kraw[rows, :]
        vwin = vbuf[rows, :DH]
        ones = jnp.ones((DH, DH), jnp.bfloat16)
        dk_sum = jnp.zeros((WIN, DH), jnp.float32)
        dv_sum = jnp.zeros((WIN, DH), jnp.float32)
        for p in range(8 // GROUP):
            q_parts, g_parts, o_parts = [], [], []
            for n in range(GROUP):
                lanes = slice((GROUP * p + n) * DH, (GROUP * p + n + 1) * DH)
                q_parts.append(qbuf[b, :, lanes])
                g_parts += [gbuf[j0, :, lanes], gbuf[j1, :, lanes]]
                o_parts += [att[2 * b, :, lanes], att[2 * b + 1, :, lanes]]
            q2 = jnp.concatenate(q_parts, axis=0)
            g2 = jnp.concatenate(g_parts, axis=0)
            o2 = jnp.concatenate(o_parts, axis=0)
            prod = (g2.astype(jnp.float32) * o2.astype(jnp.float32)).astype(jnp.bfloat16)
            delta = jnp.dot(prod, ones, preferred_element_type=jnp.float32)
            dprob = lax.dot_general(g2, vwin, dims_nt, preferred_element_type=jnp.float32)
            w = pst[b, p]
            scale = inv[b, p]
            scaled = jnp.concatenate([scale] * (WIN // DH), axis=1)
            delta = jnp.concatenate([delta] * (WIN // DH), axis=1)
            ds = (w.astype(jnp.float32) * (scaled * (dprob - delta))).astype(jnp.bfloat16)
            g2 = (g2.astype(jnp.float32) * scale).astype(jnp.bfloat16)
            dq = (jnp.dot(ds, kwin, preferred_element_type=jnp.float32) * ROOT).astype(jnp.bfloat16)
            dk_sum += lax.dot_general(ds, q2, dims_tn, preferred_element_type=jnp.float32)
            dv_sum += lax.dot_general(w, g2, dims_tn, preferred_element_type=jnp.float32)
            for n in range(GROUP):
                lanes = slice((GROUP * p + n) * DH, (GROUP * p + n + 1) * DH)
                dqs[b, :, lanes] = dq[n * BLK : (n + 1) * BLK]
        dk[rows, :] += dk_sum
        dv[rows, :] += dv_sum

    def backward_step(s):
        step, half = turn_half(s)
        b = (2 * (y + z + step) + half) % NHEAD

        @pl.when(b >= 2)
        def _():
            backward(b)

        start(copy_qg(b))

    def pass_att(s):
        m = relayed(s)
        landed(arel.at[m], r_arel.at[m])
        start(copy_af(s))

    loop(2, backward)
    start(copy_hal_k)
    start(copy_hal_v)
    loop(6, backward_step)
    loop(8, pass_att)
    loop(2, lambda n: backward_step(n + 6))

    landed(hk, r_hal.at[0])
    landed(hv, r_hal.at[1])
    k_sum = dk[pl.ds(MOST, SHARD), :]
    v_sum = dv[pl.ds(MOST, SHARD), :]
    inner = SHARD - MOST
    k_sum = jnp.concatenate([k_sum[:inner], k_sum[inner:] + hk[...]], axis=0)
    v_sum = jnp.concatenate([v_sum[:inner], v_sum[inner:] + hv[...]], axis=0)
    k_sum = jnp.dot(
        k_sum * ROOT,
        sign_grid(),
        precision=lax.Precision.HIGHEST,
        preferred_element_type=jnp.float32,
    )
    k_sum = (k_sum * ROOT).astype(jnp.bfloat16)
    v_sum = v_sum.astype(jnp.bfloat16)
    for b in range(NHEAD):
        kvst[b, 0] = k_sum[b * BLK : (b + 1) * BLK]
        kvst[b, 1] = v_sum[b * BLK : (b + 1) * BLK]
    loop(8, lambda s: start(copy_kg((2 * (y + z) + s) % NHEAD)))

    loop(4, lambda s: away(s, drain, copy_kvr))
    drain(copy_kvo())
    loop(4, lambda s: drain(copy_kva(s)))
    loop(4, lambda s: others(s, drain, copy_kvf))

    @pl.when(h >= 6)
    def _():
        loop(8, lambda s: drain(copy_edge(s)))

    loop(4, lambda s: away(s, drain, copy_qr))
    drain(copy_qo())
    loop(4, lambda s: drain(copy_qa(s)))
    loop(4, lambda s: others(s, drain, copy_qf))
    loop(16, lambda s: drain(copy_g(s)))

    @pl.when(co == 0)
    def _():
        for s in range(16):
            drain(copy_att_far(s))

    @pl.when(co == 1)
    def _():
        for s in range(16):
            drain(copy_att_near(s))

    loop(8, lambda s: drain(copy_af(s)))
    loop(8, lambda b: drain(copy_qg(b)))
    loop(8, lambda b: drain(copy_kg(b)))
    drain(copy_hal_k)
    drain(copy_hal_v)
    loop(8, lambda n: landed(kvland.at[n], r_kg.at[n]))
    for n in range(NHEAD):
        kg_o[:, n * DH : (n + 1) * DH] = kvland[n, 0]
        vg_o[:, n * DH : (n + 1) * DH] = kvland[n, 1]
    loop(8, lambda n: landed(qg_o.at[:, al(n, WIDE)], r_qg.at[n]))
    loop(16, lambda n: landed(att_o.at[al(n // 8, PIECE), al(n % 8, WIDE)], r_att.at[n]))


def local(queries, keys, values, out_grad, doc_starts, piece_order):
    any_spec = pl.BlockSpec(memory_space=pl.ANY)
    vmem = pl.BlockSpec(memory_space=pltpu.VMEM)
    smem = pl.BlockSpec(memory_space=pltpu.SMEM)
    bf, f32 = jnp.bfloat16, jnp.float32
    shapes = [
        jax.ShapeDtypeStruct(a.shape, bf) for a in (out_grad, queries, keys, values)
    ]
    dma = pltpu.SemaphoreType.DMA
    ext = SHARD + MOST
    results = pl.pallas_call(
        attention_kernel,
        out_shape=shapes,
        in_specs=[any_spec, vmem, vmem, any_spec, vmem, smem],
        out_specs=[any_spec] * 2 + [vmem] * 2,
        scratch_shapes=[
            pltpu.VMEM((NHEAD, BLK, WIDE), bf),
            pltpu.VMEM((4, BLK, WIDE), bf),
            pltpu.VMEM((NHEAD, 2, BLK, DH), bf),
            pltpu.VMEM((4, 2, BLK, DH), bf),
            pltpu.VMEM((10, 2, BLK, DH), bf),
            pltpu.VMEM((ext, DH), bf),
            pltpu.VMEM((ext, DH), bf),
            pltpu.VMEM((ext, 2 * DH), bf),
            pltpu.VMEM((NCTX, PIECE, WIDE), bf),
            pltpu.VMEM((NHEAD, 8 // GROUP, GROUP * BLK, WIN), bf),
            pltpu.VMEM((NHEAD, 8 // GROUP, GROUP * BLK, DH), f32),
            pltpu.VMEM((NCTX, PIECE, WIDE), bf),
            pltpu.VMEM((NCTX, PIECE, WIDE), bf),
            pltpu.VMEM((8, PIECE, WIDE), bf),
            pltpu.VMEM((NHEAD, BLK, WIDE), bf),
            pltpu.VMEM((ext, DH), f32),
            pltpu.VMEM((ext, DH), f32),
            pltpu.VMEM((MOST, DH), f32),
            pltpu.VMEM((MOST, DH), f32),
            pltpu.VMEM((NHEAD, 2, BLK, DH), bf),
            pltpu.VMEM((NHEAD, 2, BLK, DH), bf),
        ]
        + [dma((n,)) for n in (4, 1, 4, 4, 8, 4, 1, 4, 4, 16, 16, 8, 8, 8, 2)]
        + [dma((n,)) for n in (10, 4, 8, 4, 16, 8, 16, 8, 8, 2)],
        compiler_params=pltpu.CompilerParams(
            collective_id=0, has_side_effects=True, vmem_limit_bytes=48 * 1024 * 1024
        ),
        name="attention",
    )(
        queries, keys, values, out_grad,
        doc_starts.reshape(1, -1), piece_order,
    )
    return tuple(results)


def solution(mesh):
    rows = P(("ctx", "head"), None)
    return jax.shard_map(
        local,
        mesh=mesh,
        in_specs=(rows, rows, rows, rows, P(), P()),
        out_specs=(rows, rows, rows, rows),
        check_vma=False,
    )
```

```python
import functools
import math

import jax
import jax.numpy as jnp
from jax import lax
from jax.experimental import pallas as pl
from jax.experimental.pallas import tpu as pltpu
from jax.sharding import PartitionSpec as P

MESH = pl.DeviceIdType.MESH
DH = 128
BLK = 128
MOST = 256
WIN = MOST + BLK
PIECE = 64
SHARD = 1024
WIDE = 1024
NCTX = 16
NHEAD = 8
GROUP = 4
NEG = -1e30
MOVES = (
    (1, 1), (3, 3), (1, 3), (3, 1), (1, 0), (3, 0), (0, 1), (0, 3),
    (2, 1), (2, 3), (1, 2), (3, 2), (2, 2), (2, 0), (0, 2), (0, 0),
)
ROOT = 1.0 / math.sqrt(DH)


def sign_grid():
    common = lax.broadcasted_iota(jnp.int32, (DH, DH), 0) & lax.broadcasted_iota(jnp.int32, (DH, DH), 1)
    for shift in (4, 2, 1):
        common = common ^ (common >> shift)
    return (1 - 2 * (common & 1)).astype(jnp.float32)


def unit(shard, kv):
    even = kv % 2 == 0
    return (
        jnp.where(even, shard, (kv // 2) * 4 + shard % 4),
        jnp.where(even, kv, 2 * (shard // 4) + 1),
    )


def attention_kernel(
    q, k, v, g, docs, order,
    att_o, qg_o, kg_o, vg_o,
    qbuf, qrel, kvs, kvrel, kvbuf, kraw, kcod, vbuf, gbuf, pst, inv, att, stg, arel, dqs, dk, dv, hk, hv, kvst, kvland,
    s_kvr, s_kvo, s_kva, s_kvf, s_edge, s_qr, s_qo, s_qa, s_qf, s_g, s_att, s_af, s_qg, s_kg, s_hal,
    r_kv, r_kvrel, r_q, r_qrel, r_g, r_arel, r_att, r_qg, r_kg, r_hal,
):
    c = lax.axis_index("ctx")
    h = lax.axis_index("head")
    z, x, y, co = c // 4, c % 4, h // 2, h % 2
    shard = jnp.where(co == 0, c, y * 4 + x)
    kv = jnp.where(co == 0, 2 * y, 2 * z + 1)

    def al(index, size):
        return pl.ds(pl.multiple_of(index * size, size), size)

    def start(copy):
        src, dst, ssem, rsem, tc, th = copy
        own = (tc == c) & (th == h)

        @pl.when(own)
        def _():
            pltpu.make_async_copy(src, dst, rsem).start()

        @pl.when(jnp.logical_not(own))
        def _():
            pltpu.make_async_remote_copy(
                src, dst, ssem, rsem, device_id={"ctx": tc, "head": th}, device_id_type=MESH
            ).start()

    def drain(copy):
        src, dst, ssem, rsem, tc, th = copy
        own = (tc == c) & (th == h)

        @pl.when(jnp.logical_not(own))
        def _():
            pltpu.make_async_remote_copy(
                src, dst, ssem, rsem, device_id={"ctx": tc, "head": th}, device_id_type=MESH
            ).wait_send()

    def landed(ref, sem):
        pltpu.make_async_copy(ref, ref, sem).wait()

    def loop(count, body):
        def step(s, carry):
            body(s)
            return carry

        lax.fori_loop(0, count, step, 0)

    def turn(s):
        return jnp.where(s < 2, 1 + 2 * s, 6 - 2 * s)

    def turn_half(s):
        return jnp.where(s < 4, 1 + 2 * (s % 2), 2 - 2 * (s % 2)), s // 2 % 2

    def far(s):
        return (z + 8 - y - turn(s)) % 4

    def near(s):
        return (y + z + turn(s)) % 4

    def copy_kvr(s):
        to = far(s)
        return (kvs.at[2 * to + 1], kvrel.at[z], s_kvr.at[s], r_kvrel.at[z], to * 4 + x, h)

    def copy_kvo():
        return (kvs.at[2 * z + 1], kvbuf.at[h + 2], s_kvo.at[0], r_kv.at[h + 2], c, 2 * z + 1)

    def copy_kva(s):
        to = 2 * ((y + turn(s)) % 4)
        return (kvs.at[to], kvbuf.at[h + 2], s_kva.at[s], r_kv.at[h + 2], c, to)

    def copy_kvf(s):
        src = near(s)
        return (kvrel.at[src], kvbuf.at[h + 2], s_kvf.at[s], r_kv.at[h + 2], c, 2 * src + 1)

    def copy_edge(s):
        kk = (h + s) % NHEAD
        return (kvs.at[kk], kvbuf.at[h % 2], s_edge.at[s], r_kv.at[h % 2]) + unit((c + 1) % NCTX, kk)

    def copy_qr(s):
        to = far(s)
        return (q.at[:, al(2 * to + 1, WIDE)], qrel.at[z], s_qr.at[s], r_qrel.at[z], to * 4 + x, h)

    def copy_qo():
        return (q.at[:, al(2 * z + 1, WIDE)], qbuf.at[h], s_qo.at[0], r_q.at[h], c, 2 * z + 1)

    def copy_qa(s):
        to = 2 * ((y + turn(s)) % 4)
        return (q.at[:, al(to, WIDE)], qbuf.at[h], s_qa.at[s], r_q.at[h], c, to)

    def copy_qf(s):
        src = near(s)
        return (qrel.at[src], qbuf.at[h], s_qf.at[s], r_q.at[h], c, 2 * src + 1)

    def copy_g(s):
        step, half = turn_half(s % 8)
        step = jnp.where(s >= 8, step, 3 - step)
        half = (half + x) % 2
        kk = jnp.where(s >= 8, 2 * ((y + z + step) % 4), 2 * ((z + step) % 4) + 1)
        src = g.at[al(half, PIECE), al(kk, WIDE)]
        return (src, gbuf.at[c], s_g.at[s], r_g.at[c]) + unit(2 * h + half, kk)

    def copy_att_far(s):
        j = (z + 8 - y - MOVES[s][0]) % 4 * 4 + (x + MOVES[s][1]) % 4
        slot = z * 2 + x % 2
        return (stg.at[j], arel.at[slot], s_att.at[s], r_arel.at[slot], j, 2 * y + x // 2)

    def copy_att_near(s):
        j = (z + MOVES[s][0]) % 4 * 4 + (x + MOVES[s][1]) % 4
        dst = att_o.at[al(x % 2, PIECE), al(kv, WIDE)]
        return (stg.at[j], dst, s_att.at[s], r_att.at[(x % 2) * 8 + kv], j, 2 * y + x // 2)

    def relayed(s):
        step, half = turn_half(s)
        step = jnp.where(s < 4, step, 2 - step)
        return ((y + z + step) % 4) * 2 + half

    def copy_af(s):
        m = relayed(s)
        dst = att_o.at[al(m % 2, PIECE), al(2 * y, WIDE)]
        return (arel.at[m], dst, s_af.at[s], r_att.at[(m % 2) * 8 + 2 * y], c, 2 * (m // 2) + co)

    def copy_qg(b):
        return (dqs.at[b], qg_o.at[:, al(kv, WIDE)], s_qg.at[b], r_qg.at[kv], shard, b)

    def copy_kg(b):
        return (kvst.at[b], kvland.at[kv], s_kg.at[b], r_kg.at[kv], shard, b)

    back = unit((shard + NCTX - 1) % NCTX, kv)
    copy_hal_k = (dk.at[pl.ds(0, MOST)], hk, s_hal.at[0], r_hal.at[0]) + back
    copy_hal_v = (dv.at[pl.ds(0, MOST)], hv, s_hal.at[1], r_hal.at[1]) + back

    barrier = pltpu.get_barrier_semaphore()

    def greet(t):
        pl.semaphore_signal(
            barrier, inc=1, device_id={"ctx": t // NHEAD, "head": t % NHEAD}, device_id_type=MESH
        )

    loop(NCTX * NHEAD, greet)
    for n in range(NHEAD):
        kvs[n, 0] = k[:, n * DH : (n + 1) * DH]
        kvs[n, 1] = v[:, n * DH : (n + 1) * DH]
    dk[...] = jnp.zeros_like(dk)
    dv[...] = jnp.zeros_like(dv)
    vbuf[:, DH:] = jnp.ones_like(vbuf[:, DH:])
    pl.semaphore_wait(barrier, NCTX * NHEAD)

    def away(s, act, copy):
        @pl.when(far(s) != z)
        def _():
            act(copy(s))

    def others(s, act, copy):
        @pl.when(near(s) != z)
        def _():
            act(copy(s))

    loop(4, lambda s: away(s, start, copy_qr))
    loop(4, lambda s: start(copy_qa(s)))
    start(copy_qo())
    loop(4, lambda s: away(s, start, copy_kvr))
    loop(4, lambda s: start(copy_kva(s)))
    start(copy_kvo())

    @pl.when(h >= 6)
    def _():
        loop(8, lambda s: start(copy_edge(s)))

    def pass_on(s):
        src = near(s)

        @pl.when(src != z)
        def _():
            landed(qrel.at[src], r_qrel.at[src])
            start(copy_qf(s))
            landed(kvrel.at[src], r_kvrel.at[src])
            start(copy_kvf(s))

    loop(4, pass_on)
    loop(16, lambda s: start(copy_g(s)))

    starts = docs[...].astype(jnp.float32)

    loop(10, lambda n: landed(kvbuf.at[n], r_kv.at[n]))
    for n in range(10):
        kraw[n * BLK : (n + 1) * BLK] = kvbuf[n, 0]
        vbuf[n * BLK : (n + 1) * BLK, :DH] = kvbuf[n, 1]
    turned = jnp.dot(kraw[...], sign_grid().astype(jnp.bfloat16), preferred_element_type=jnp.float32)
    kcod[...] = (turned * ROOT).astype(jnp.bfloat16)

    def pair(block, p):
        parts = [block[:, (GROUP * p + n) * DH : (GROUP * p + n + 1) * DH] for n in range(GROUP)]
        return jnp.concatenate(parts, axis=0)

    dims_nt = (((1,), (1,)), ((), ()))
    dims_tn = (((0,), (0,)), ((), ()))

    def forward(s):
        b = (h + 8 - s) % NHEAD
        row = lax.broadcasted_iota(jnp.int32, (BLK, 1), 0) + (shard * SHARD + b * BLK)
        rowf = row.astype(jnp.float32)
        begin = jnp.max(jnp.where(starts <= rowf, starts, 0.0), axis=1, keepdims=True)
        col = lax.broadcasted_iota(jnp.int32, (BLK, WIN), 1) + (shard * SHARD + b * BLK - MOST)
        colf = col.astype(jnp.float32)
        bias = jnp.where((colf <= rowf) & (colf >= begin), 0.0, NEG)
        bias = jnp.concatenate([bias] * GROUP, axis=0)
        kwin = kcod[pl.ds(pl.multiple_of(b * BLK, BLK), WIN), :]
        vwin = vbuf[pl.ds(pl.multiple_of(b * BLK, BLK), WIN), :]
        for p in range(8 // GROUP):
            q2 = jnp.concatenate(
                [qbuf[b, :, (GROUP * p + n) * DH : (GROUP * p + n + 1) * DH] for n in range(GROUP)], axis=0
            )
            score = lax.dot_general(q2, kwin, dims_nt, preferred_element_type=jnp.float32)
            score = score * (ROOT * math.log2(math.e)) + bias
            top = jnp.max(score, axis=1, keepdims=True)
            w = jnp.exp2(score - top).astype(jnp.bfloat16)
            pst[b, p] = w
            both = jnp.dot(w, vwin, preferred_element_type=jnp.float32)
            scale = 1.0 / both[:, DH:]
            inv[b, p] = scale
            out = (both[:, :DH] * scale).astype(jnp.bfloat16)
            for n in range(GROUP):
                lanes = slice((GROUP * p + n) * DH, (GROUP * p + n + 1) * DH)
                att[2 * b, :, lanes] = out[n * BLK : n * BLK + PIECE]
                att[2 * b + 1, :, lanes] = out[n * BLK + PIECE : (n + 1) * BLK]

    loop(8, lambda b: landed(qbuf.at[b], r_q.at[b]))
    loop(8, forward)

    def fill(j):
        stg[j] = att[order[shard, j]]

    loop(16, fill)

    def send_att(s):
        @pl.when(co == 0)
        def _():
            start(copy_att_far(s))

        @pl.when(co == 1)
        def _():
            start(copy_att_near(s))

    for s in range(16):
        send_att(s)
    loop(16, lambda j: landed(gbuf.at[j], r_g.at[j]))

    def where_from(piece):
        def look(j, found):
            return jnp.where(order[shard, j] == piece, j, found)

        return lax.fori_loop(0, NCTX, look, 0)

    def backward(b):
        j0 = where_from(2 * b)
        j1 = where_from(2 * b + 1)
        rows = pl.ds(pl.multiple_of(b * BLK, BLK), WIN)
        kwin = kraw[rows, :]
        vwin = vbuf[rows, :DH]
        ones = jnp.ones((DH, DH), jnp.bfloat16)
        dk_sum = jnp.zeros((WIN, DH), jnp.float32)
        dv_sum = jnp.zeros((WIN, DH), jnp.float32)
        for p in range(8 // GROUP):
            q_parts, g_parts, o_parts = [], [], []
            for n in range(GROUP):
                lanes = slice((GROUP * p + n) * DH, (GROUP * p + n + 1) * DH)
                q_parts.append(qbuf[b, :, lanes])
                g_parts += [gbuf[j0, :, lanes], gbuf[j1, :, lanes]]
                o_parts += [att[2 * b, :, lanes], att[2 * b + 1, :, lanes]]
            q2 = jnp.concatenate(q_parts, axis=0)
            g2 = jnp.concatenate(g_parts, axis=0)
            o2 = jnp.concatenate(o_parts, axis=0)
            prod = (g2.astype(jnp.float32) * o2.astype(jnp.float32)).astype(jnp.bfloat16)
            delta = jnp.dot(prod, ones, preferred_element_type=jnp.float32)
            dprob = lax.dot_general(g2, vwin, dims_nt, preferred_element_type=jnp.float32)
            w = pst[b, p]
            scale = inv[b, p]
            scaled = jnp.concatenate([scale] * (WIN // DH), axis=1)
            delta = jnp.concatenate([delta] * (WIN // DH), axis=1)
            ds = (w.astype(jnp.float32) * (scaled * (dprob - delta))).astype(jnp.bfloat16)
            g2 = (g2.astype(jnp.float32) * scale).astype(jnp.bfloat16)
            dq = (jnp.dot(ds, kwin, preferred_element_type=jnp.float32) * ROOT).astype(jnp.bfloat16)
            dk_sum += lax.dot_general(ds, q2, dims_tn, preferred_element_type=jnp.float32)
            dv_sum += lax.dot_general(w, g2, dims_tn, preferred_element_type=jnp.float32)
            for n in range(GROUP):
                lanes = slice((GROUP * p + n) * DH, (GROUP * p + n + 1) * DH)
                dqs[b, :, lanes] = dq[n * BLK : (n + 1) * BLK]
        dk[rows, :] += dk_sum
        dv[rows, :] += dv_sum

    def backward_step(s):
        step, half = turn_half(s)
        b = (2 * (y + z + step) + half) % NHEAD

        @pl.when(b >= 2)
        def _():
            backward(b)

        start(copy_qg(b))

    def pass_att(s):
        m = relayed(s)
        landed(arel.at[m], r_arel.at[m])
        start(copy_af(s))

    loop(2, backward)
    start(copy_hal_k)
    start(copy_hal_v)
    loop(6, backward_step)
    loop(8, pass_att)
    loop(2, lambda n: backward_step(n + 6))

    landed(hk, r_hal.at[0])
    landed(hv, r_hal.at[1])
    k_sum = dk[pl.ds(MOST, SHARD), :]
    v_sum = dv[pl.ds(MOST, SHARD), :]
    inner = SHARD - MOST
    k_sum = jnp.concatenate([k_sum[:inner], k_sum[inner:] + hk[...]], axis=0)
    v_sum = jnp.concatenate([v_sum[:inner], v_sum[inner:] + hv[...]], axis=0)
    k_sum = jnp.dot(
        k_sum * ROOT,
        sign_grid(),
        precision=lax.Precision.HIGHEST,
        preferred_element_type=jnp.float32,
    )
    k_sum = (k_sum * ROOT).astype(jnp.bfloat16)
    v_sum = v_sum.astype(jnp.bfloat16)
    for b in range(NHEAD):
        kvst[b, 0] = k_sum[b * BLK : (b + 1) * BLK]
        kvst[b, 1] = v_sum[b * BLK : (b + 1) * BLK]
    loop(8, lambda s: start(copy_kg((2 * (y + z) + s) % NHEAD)))

    loop(4, lambda s: away(s, drain, copy_kvr))
    drain(copy_kvo())
    loop(4, lambda s: drain(copy_kva(s)))
    loop(4, lambda s: others(s, drain, copy_kvf))

    @pl.when(h >= 6)
    def _():
        loop(8, lambda s: drain(copy_edge(s)))

    loop(4, lambda s: away(s, drain, copy_qr))
    drain(copy_qo())
    loop(4, lambda s: drain(copy_qa(s)))
    loop(4, lambda s: others(s, drain, copy_qf))
    loop(16, lambda s: drain(copy_g(s)))

    @pl.when(co == 0)
    def _():
        for s in range(16):
            drain(copy_att_far(s))

    @pl.when(co == 1)
    def _():
        for s in range(16):
            drain(copy_att_near(s))

    loop(8, lambda s: drain(copy_af(s)))
    loop(8, lambda b: drain(copy_qg(b)))
    loop(8, lambda b: drain(copy_kg(b)))
    drain(copy_hal_k)
    drain(copy_hal_v)
    loop(8, lambda n: landed(kvland.at[n], r_kg.at[n]))
    for n in range(NHEAD):
        kg_o[:, n * DH : (n + 1) * DH] = kvland[n, 0]
        vg_o[:, n * DH : (n + 1) * DH] = kvland[n, 1]
    loop(8, lambda n: landed(qg_o.at[:, al(n, WIDE)], r_qg.at[n]))
    loop(16, lambda n: landed(att_o.at[al(n // 8, PIECE), al(n % 8, WIDE)], r_att.at[n]))


def local(queries, keys, values, out_grad, doc_starts, piece_order):
    any_spec = pl.BlockSpec(memory_space=pl.ANY)
    vmem = pl.BlockSpec(memory_space=pltpu.VMEM)
    smem = pl.BlockSpec(memory_space=pltpu.SMEM)
    bf, f32 = jnp.bfloat16, jnp.float32
    shapes = [
        jax.ShapeDtypeStruct(a.shape, bf) for a in (out_grad, queries, keys, values)
    ]
    dma = pltpu.SemaphoreType.DMA
    ext = SHARD + MOST
    results = pl.pallas_call(
        attention_kernel,
        out_shape=shapes,
        in_specs=[any_spec, vmem, vmem, any_spec, vmem, smem],
        out_specs=[any_spec] * 2 + [vmem] * 2,
        scratch_shapes=[
            pltpu.VMEM((NHEAD, BLK, WIDE), bf),
            pltpu.VMEM((4, BLK, WIDE), bf),
            pltpu.VMEM((NHEAD, 2, BLK, DH), bf),
            pltpu.VMEM((4, 2, BLK, DH), bf),
            pltpu.VMEM((10, 2, BLK, DH), bf),
            pltpu.VMEM((ext, DH), bf),
            pltpu.VMEM((ext, DH), bf),
            pltpu.VMEM((ext, 2 * DH), bf),
            pltpu.VMEM((NCTX, PIECE, WIDE), bf),
            pltpu.VMEM((NHEAD, 8 // GROUP, GROUP * BLK, WIN), bf),
            pltpu.VMEM((NHEAD, 8 // GROUP, GROUP * BLK, DH), f32),
            pltpu.VMEM((NCTX, PIECE, WIDE), bf),
            pltpu.VMEM((NCTX, PIECE, WIDE), bf),
            pltpu.VMEM((8, PIECE, WIDE), bf),
            pltpu.VMEM((NHEAD, BLK, WIDE), bf),
            pltpu.VMEM((ext, DH), f32),
            pltpu.VMEM((ext, DH), f32),
            pltpu.VMEM((MOST, DH), f32),
            pltpu.VMEM((MOST, DH), f32),
            pltpu.VMEM((NHEAD, 2, BLK, DH), bf),
            pltpu.VMEM((NHEAD, 2, BLK, DH), bf),
        ]
        + [dma((n,)) for n in (4, 1, 4, 4, 8, 4, 1, 4, 4, 16, 16, 8, 8, 8, 2)]
        + [dma((n,)) for n in (10, 4, 8, 4, 16, 8, 16, 8, 8, 2)],
        compiler_params=pltpu.CompilerParams(
            collective_id=0, has_side_effects=True, vmem_limit_bytes=48 * 1024 * 1024
        ),
        name="attention",
    )(
        queries, keys, values, out_grad,
        doc_starts.reshape(1, -1), piece_order,
    )
    return tuple(results)


def solution(mesh):
    rows = P(("ctx", "head"), None)
    return jax.shard_map(
        local,
        mesh=mesh,
        in_specs=(rows, rows, rows, rows, P(), P()),
        out_specs=(rows, rows, rows, rows),
        check_vma=False,
    )
```
